32 devices in a mesh: groups: 2 (over y), tgt: 4 (over z), src: 2 (over x), sub: 2 (over core).
Axes of the slice: x: 2, y: 2, z: 4, core: 2. Of those that a mesh axis runs over, the one named last changes fastest.
Arguments:
- points: float32 [3, 4096], P(None, ('groups', 'tgt', 'src', 'sub')), parts along dimension 1, may hold values from -1.4 to 1.4, as said below
- density: float32 [32, 4096], P(None, ('groups', 'tgt', 'src', 'sub')), parts along dimension 1, may hold values from 0.2 to 2
- incident: float32 [32, 4096], P(None, ('groups', 'tgt', 'src', 'sub')), parts along dimension 1, may hold values from -0.21 to 0.21
- precond: float32 [4096], P(('groups', 'tgt', 'src', 'sub')), parts along dimension 0, may hold values from 0.054414064 to 0.16324219
- receivers: int32 [4096], P('groups'), parts along dimension 0, may hold values from 0 to 65535
Outputs:
- density_out: float32 [32, 4096], P(None, ('groups', 'tgt', 'src', 'sub')), parts along dimension 1
- far_field: float32 [32, 4096], P(None, ('groups', 'tgt', 'src', 'sub')), parts along dimension 1
The draws below stay inside these ranges and needn't reach their ends.
There are 2 independent parts, one for each index of `groups`. The reference program is written for one: setup_inputs(seed, part) draws one part's arguments, and reference() takes and returns one part's arrays. A program takes and returns all parts, laid end to end along the dimension named above; each array names one. Nothing has to cross between parts.
Inputs may be any that keep to these rules, and one draw needn't show every extreme that they name: Coordinates of points of a closed star-shaped surface around the anchor. `receivers`: numbers of directions in the receiver table.
All inputs are finite; a program needn't handle non-finite values.
Results may differ from the reference program's by a relative error of at most 0.0015.
Values may be sent and summed in bfloat16 or wider, within the bound.
No kernel may reach another device: no remote copies, remote signals or barrier semaphores. Data moves between devices by JAX's collectives and lax.ppermute only.
A program may use at most 64 MiB of HBM per device.

```python
import math
import jax
import jax.numpy as jnp
from jax import lax

C = 32
PTS_DEV = 128
ITERS = 4
NDIR = 65536
NPTS = 2048
NRCV = 2048


def draw_points(key, part):
    shift_key, phase_key = jax.random.split(jax.random.fold_in(key, 17), 2)
    position = jnp.arange(NPTS)
    patches = NPTS // PTS_DEV
    patch = (position // PTS_DEV).astype(jnp.float32)
    height = 1.0 - (2.0 * patch + 1.0) / patches
    radial = jnp.sqrt(jnp.maximum(1.0 - height * height, 0.0))
    azimuth = patch * 2.399963
    center = jnp.stack([radial * jnp.cos(azimuth), radial * jnp.sin(azimuth), height])
    spread = min(1.6 / math.sqrt(patches), 0.15)
    offsets = jax.random.truncated_normal(shift_key, -3.0, 3.0, (3, NPTS), jnp.float32) * spread
    moved = center + offsets
    unit = moved / jnp.sqrt(jnp.sum(moved * moved, axis=0, keepdims=True))
    phases = jax.random.uniform(phase_key, (3,), jnp.float32, 0.0, 6.283)
    amplitude = 0.12
    radius = 1.0 + amplitude * jnp.sin(3.0 * unit[0] + phases[0]) * jnp.cos(2.0 * unit[1] + phases[1])
    radius = radius + 0.5 * amplitude * jnp.sin(4.0 * unit[2] + phases[2])
    return (unit * radius[None, :]).astype(jnp.float32)


def touch_ends(drawn, key, least, largest):
    longest = drawn.shape.index(max(drawn.shape))
    spots = []
    for shift in (0, 1):
        where = [jax.random.randint(jax.random.fold_in(key, axis), (), 0, length) for axis, length in enumerate(drawn.shape)]
        where[longest] = (where[longest] + shift) % drawn.shape[longest]
        spots.append(tuple(where))
    return drawn.at[spots[0]].set(least).at[spots[1]].set(largest)


def level_of(rng, dims, shards, low, top_value):
    gain, own = 1.0, jax.random.fold_in(rng, 6)
    for dim, shards_of in shards:
        steps = jnp.exp(jax.random.uniform(jax.random.fold_in(own, dim), (shards_of,), jnp.float32, low / len(shards), top_value / len(shards)))
        gain = gain * jnp.repeat(steps, dims[dim] // shards_of).reshape([-1 if axis == dim else 1 for axis in range(len(dims))])
    return gain


def noise(rng, shape, width, limit, cuts=(), held_as=jnp.bfloat16):
    entries = width * jax.random.normal(rng, shape, jnp.float32)
    if cuts:
        entries = entries * level_of(rng, shape, cuts, -0.22, 0.18)
    return jnp.clip(entries, -limit, limit).astype(held_as)


def setup_inputs(seed: int = 0, part: int = 0) -> dict:
    arg_keys = jax.random.split(jax.random.key(seed), 6)
    own_keys = jax.random.split(jax.random.fold_in(arg_keys[5], part), 6)
    return {
        "points": draw_points(jax.random.fold_in(jax.random.fold_in(arg_keys[5], part), 71), part),
        "density": jnp.clip(0.2 + 1.8 * jax.random.uniform(own_keys[1], (C, NPTS), jnp.float32) ** level_of(own_keys[1], (C, NPTS), ((1, 16),), -0.2, 0.2), 0.2, 2.0),
        "incident": noise(own_keys[2], (C, NPTS), 0.035, 0.21, ((1, 16),), jnp.float32),
        "precond": jnp.clip(jnp.exp(math.log(0.16324219) - 1.0986123 * jax.random.uniform(own_keys[3], (NPTS,), jnp.float32) ** level_of(own_keys[3], (NPTS,), ((0, 16),), -0.2, 0.2)), 0.054414064, 0.16324219),
        "receivers": touch_ends(jax.random.randint(own_keys[4], (NRCV,), 0, NDIR), jax.random.fold_in(own_keys[4], 1), 0, NDIR - 1).astype(jnp.int32),
    }


WAVENUMBER = 32.0
SMOOTHING = 0.02
FOUR_PI = 4.0 * math.pi

def single_layer(targets, sources):
    delta_x = targets[0][:, None] - sources[0][None, :]
    delta_y = targets[1][:, None] - sources[1][None, :]
    delta_z = targets[2][:, None] - sources[2][None, :]
    squared = delta_x * delta_x + delta_y * delta_y + delta_z * delta_z
    values = jnp.cos(WAVENUMBER * jnp.sqrt(squared)) / (FOUR_PI * jnp.sqrt(squared + SMOOTHING * SMOOTHING))
    return values.astype(jnp.bfloat16)

def far_kernel(toward, sources):
    projection = toward[0][:, None] * sources[0][None, :] + toward[1][:, None] * sources[1][None, :]
    projection = projection + toward[2][:, None] * sources[2][None, :]
    return jnp.cos(WAVENUMBER * projection).astype(jnp.bfloat16)

def receiver_directions(direction_index):
    upper_part = direction_index // 256
    lower_part = direction_index % 256
    rotation = (upper_part * 14080 + lower_part * 40503) % 65536
    azimuth = rotation.astype(jnp.float32) * (2.0 * math.pi / 65536.0)
    height = 1.0 - (2 * direction_index + 1).astype(jnp.float32) / NDIR
    radial = jnp.sqrt(jnp.maximum(1.0 - height * height, 0.0))
    return jnp.stack([radial * jnp.cos(azimuth), radial * jnp.sin(azimuth), height])

def contract(weighted, kernel_table):
    return lax.dot_general(weighted, kernel_table, (((1,), (1,)), ((), ())), preferred_element_type=jnp.float32)

def blocked(weighted, targets, sources, maker):
    target_count = targets.shape[1]
    block_width = math.gcd(target_count, 1024)
    target_blocks = targets.reshape(3, target_count // block_width, block_width).transpose(1, 0, 2)

    def one_block(target_rows):
        return contract(weighted, maker(target_rows, sources))
    result = lax.map(one_block, target_blocks)
    return result.transpose(1, 0, 2).reshape(weighted.shape[0], target_count)

def reference(points, density, incident, precond, receivers):
    point_count = points.shape[1]
    cell_area = FOUR_PI / point_count
    for iteration in range(ITERS):
        weighted = (density * cell_area).astype(jnp.bfloat16)
        field = blocked(weighted, points, points, single_layer)
        density = density - (field + incident) / precond[None, :]
    weighted = (density * cell_area).astype(jnp.bfloat16)
    toward = receiver_directions(receivers)
    far_field = blocked(weighted, toward, points, far_kernel)
    return (density, far_field)
```

```python
import math

import jax
import jax.numpy as jnp
from jax import lax
from jax.experimental import pallas as pl
from jax.experimental.pallas import tpu as pltpu
from jax.sharding import PartitionSpec as P

ITERS = 4
NDIR = 65536


WAVENUMBER = 32.0
SMOOTHING = 0.02
FOUR_PI = 4.0 * math.pi

TURNS = WAVENUMBER / (2.0 * math.pi)
SMOOTH_TURNS = (SMOOTHING * TURNS) ** 2
BLOCK = 256
TABLE_LIMIT = 24 * 2**20
VMEM_LIMIT = 56 * 2**20


def sine_coefficients(count):
    nodes = [0.03125 + 0.03125 * math.cos(math.pi * (k + 0.5) / count) for k in range(count)]
    values = [math.sin(2.0 * math.pi * math.sqrt(u)) / math.sqrt(u) for u in nodes]
    divided = list(values)
    for level in range(1, count):
        for k in range(count - 1, level - 1, -1):
            divided[k] = (divided[k] - divided[k - 1]) / (nodes[k] - nodes[k - level])
    poly = [0.0] * count
    for k in range(count - 1, -1, -1):
        shifted = [0.0] + poly[:-1]
        poly = [s - nodes[k] * p for s, p in zip(shifted, poly)]
        poly[0] += divided[k]
    return poly


SINE = sine_coefficients(4)


def cos_turns(turns, scale):
    folded = 0.25 - jnp.abs(turns - jnp.round(turns))
    square = folded * folded
    value = SINE[-1] * scale
    for c in SINE[-2::-1]:
        value = value * square + c * scale
    return value * folded


def green(squared):
    kept = jnp.maximum(squared, 1e-12)
    turns = kept * lax.rsqrt(kept)
    return (cos_turns(turns, TURNS / FOUR_PI) * lax.rsqrt(squared + SMOOTH_TURNS)).astype(jnp.bfloat16)


def split3(x):
    high = x.astype(jnp.bfloat16).astype(jnp.float32)
    rest = x - high
    mid = rest.astype(jnp.bfloat16).astype(jnp.float32)
    low = (rest - mid).astype(jnp.bfloat16).astype(jnp.float32)
    return high, mid, low


def replicated_kernel(counts, *refs):
    blocks, points_row, columns = counts
    data = refs[:blocks]
    toward_ref = refs[blocks]
    density_out, far_out = refs[blocks + 1 : blocks + 3]
    lhs, rhs, table, half_table, plane, dens, inc = refs[blocks + 3 : blocks + 10]
    stage = refs[blocks + 10 :]
    total = blocks * BLOCK
    shards_per_block = data[0].shape[0]
    width = data[0].shape[2]
    full = blocks // 2

    def lanes(start, count):
        return jnp.concatenate(
            [data[b][s, start : start + count, :] for b in range(blocks) for s in range(shards_per_block)], axis=1
        )

    head = lanes(0, 8)
    coords = head[0:3] * TURNS
    inverse = 1.0 / head[3:4]
    dens[...] = lanes(8, columns)
    inc[...] = lanes(8 + columns, columns)

    ones = jnp.ones((1, total), jnp.float32)
    left, right = [], []
    for k in range(3):
        h, m, l = split3(coords[k : k + 1])
        left += [-2.0 * h, -2.0 * h, -2.0 * m, -2.0 * m, -2.0 * h, -2.0 * l]
        right += [h, m, h, m, l, h]
    norm = coords[0:1] * coords[0:1] + coords[1:2] * coords[1:2] + coords[2:3] * coords[2:3]
    h, m, l = split3(norm)
    left += [h, m, l, ones, ones, ones]
    right += [ones, ones, ones, h, m, l]
    zeros = jnp.zeros((8, total), jnp.float32)
    left = jnp.concatenate(left + [zeros], axis=0)
    rhs[...] = jnp.concatenate(right + [zeros], axis=0).astype(jnp.bfloat16)
    lhs[...] = left.T.astype(jnp.bfloat16)

    def distances(row, count, column):
        return lax.dot_general(
            lhs[pl.ds(pl.multiple_of(row, 128), count), :],
            rhs[:, pl.ds(pl.multiple_of(column, BLOCK), BLOCK)],
            (((1,), (0,)), ((), ())),
            preferred_element_type=jnp.float32,
        )

    def fill(block, d, source):
        for r in range(0, BLOCK, 32):
            table[block, d, r : r + 32, :] = green(source[r : r + 32, :])

    stage[0][...] = distances(0, BLOCK, 0)

    def one_row(block, carry):
        for d in range(1, full):
            stage[d][...] = distances(block * BLOCK, BLOCK, lax.rem(block + d, blocks) * BLOCK)
            fill(block, d - 1, stage[d - 1])
        low = lax.rem(block, full)
        part = block // full
        stage[full][...] = distances(low * BLOCK + part * 128, 128, (low + full) * BLOCK)
        fill(block, full - 1, stage[full - 1])
        following = lax.rem(block + 1, blocks) * BLOCK
        stage[0][...] = distances(following, BLOCK, following)
        base = pl.multiple_of(part * 128, 128)
        for r in range(0, 128, 32):
            half_table[low, pl.ds(base + r, 32), :] = green(stage[full][r : r + 32, :])
        return carry

    lax.fori_loop(0, blocks, one_row, 0)

    toward = toward_ref[...].T
    for b in range(blocks):
        span = slice(b * BLOCK, (b + 1) * BLOCK)
        phase = toward[:, 0:1] * coords[0:1, span] + toward[:, 1:2] * coords[1:2, span]
        phase = phase + toward[:, 2:3] * coords[2:3, span]
        plane[:, span] = cos_turns(phase, 1.0).astype(jnp.bfloat16)

    cell_area = FOUR_PI / total

    def rounded():
        return (dens[...] * cell_area).astype(jnp.bfloat16)

    def product(w, b, kernel_block, dim):
        return lax.dot_general(
            w[:, b * BLOCK : (b + 1) * BLOCK],
            kernel_block,
            (((1,), (dim,)), ((), ())),
            preferred_element_type=jnp.float32,
        )

    def iterate(step, carry):
        w = rounded()
        for b in range(blocks):
            field = product(w, b, table[b, 0], 1)
            for d in range(1, full):
                field += product(w, (b + d) % blocks, table[b, d], 1)
                field += product(w, (b - d) % blocks, table[(b - d) % blocks, d], 0)
            if b < full:
                field += product(w, b + full, half_table[b], 1)
            else:
                field += product(w, b - full, half_table[b - full], 0)
            span = slice(b * BLOCK, (b + 1) * BLOCK)
            dens[:, span] = dens[:, span] - (field + inc[:, span]) * inverse[:, span]
        return carry

    lax.fori_loop(0, ITERS, iterate, 0)
    density_out[...] = dens[:, 0:width]
    w = rounded()
    far_out[...] = lax.dot_general(
        w, plane[...], (((1,), (1,)), ((), ())), preferred_element_type=jnp.float32
    )


def replicated_shards(points, density, incident, precond, receivers):
    count_tgt = lax.axis_size("tgt")
    count_src = lax.axis_size("src")
    count_sub = lax.axis_size("sub")
    chips = count_tgt * count_src
    columns, width = density.shape
    names = ("tgt", "src", "sub")
    payload = jnp.concatenate(
        [points, precond[None, :], jnp.zeros((4, width), jnp.float32), density, incident], axis=0
    )
    swap = [(0, 1), (1, 0)]
    own = jnp.stack([payload, lax.ppermute(payload, "sub", swap)])

    def fetch(offsets):
        pairs = [(q * 2 + c, (q ^ offsets[c]) * 2 + c) for q in range(chips) for c in range(2)]
        return lax.ppermute(own, names, pairs)

    held = [own]
    for k in range(1, chips - 1, 2):
        near = fetch((k, k + 1))
        held += [near, lax.ppermute(near, "sub", swap)]
    held.append(fetch((chips - 1, chips - 1)))

    place = (lax.axis_index("tgt") * count_src + lax.axis_index("src")) * count_sub + lax.axis_index("sub")
    rows = receivers.shape[0] // (chips * count_sub)
    toward = receiver_directions(lax.dynamic_slice_in_dim(receivers, place * rows, rows, 0))
    toward = jnp.concatenate([toward, jnp.zeros((5, rows), jnp.float32)], axis=0)

    blocks = len(held)
    total = blocks * BLOCK
    full = blocks // 2
    vmem = pl.BlockSpec(memory_space=pltpu.VMEM)
    return pl.pallas_call(
        lambda *refs: replicated_kernel((blocks, 8, columns), *refs),
        out_shape=(
            jax.ShapeDtypeStruct((columns, width), jnp.float32),
            jax.ShapeDtypeStruct((columns, rows), jnp.float32),
        ),
        in_specs=[vmem] * (blocks + 1),
        out_specs=(vmem, vmem),
        scratch_shapes=[
            pltpu.VMEM((total, 32), jnp.bfloat16),
            pltpu.VMEM((32, total), jnp.bfloat16),
            pltpu.VMEM((blocks, full, BLOCK, BLOCK), jnp.bfloat16),
            pltpu.VMEM((full, BLOCK, BLOCK), jnp.bfloat16),
            pltpu.VMEM((rows, total), jnp.bfloat16),
            pltpu.VMEM((columns, total), jnp.float32),
            pltpu.VMEM((columns, total), jnp.float32),
        ]
        + [pltpu.VMEM((BLOCK, BLOCK), jnp.float32) for _ in range(full)]
        + [pltpu.VMEM((128, BLOCK), jnp.float32)],
        compiler_params=pltpu.CompilerParams(vmem_limit_bytes=VMEM_LIMIT),
        name="iterate",
    )(*held, toward)


def single_layer(targets, sources):
    delta_x = targets[0][:, None] - sources[0][None, :]
    delta_y = targets[1][:, None] - sources[1][None, :]
    delta_z = targets[2][:, None] - sources[2][None, :]
    squared = delta_x * delta_x + delta_y * delta_y + delta_z * delta_z
    values = jnp.cos(WAVENUMBER * jnp.sqrt(squared)) / (
        FOUR_PI * jnp.sqrt(squared + SMOOTHING * SMOOTHING)
    )
    return values.astype(jnp.bfloat16)


def far_kernel(toward, sources):
    projection = toward[0][:, None] * sources[0][None, :] + toward[1][:, None] * sources[1][None, :]
    projection = projection + toward[2][:, None] * sources[2][None, :]
    return jnp.cos(WAVENUMBER * projection).astype(jnp.bfloat16)


def receiver_directions(direction_index):
    upper_part = direction_index // 256
    lower_part = direction_index % 256
    rotation = (upper_part * 14080 + lower_part * 40503) % 65536
    azimuth = rotation.astype(jnp.float32) * (2.0 * math.pi / 65536.0)
    height = 1.0 - (2 * direction_index + 1).astype(jnp.float32) / NDIR
    radial = jnp.sqrt(jnp.maximum(1.0 - height * height, 0.0))
    return jnp.stack([radial * jnp.cos(azimuth), radial * jnp.sin(azimuth), height])


def fold_blocks(running, incoming, coordinates, targets, maker):
    length = incoming.shape[1]
    block_width = math.gcd(length, 1024)

    def fold_one_block(number, accumulated):
        inside = number * block_width
        part_density = lax.dynamic_slice_in_dim(incoming, inside, block_width, 1)
        part_points = lax.dynamic_slice_in_dim(coordinates, inside, block_width, 1)
        kernel_table = maker(targets, part_points)
        return accumulated + lax.dot_general(
            part_density, kernel_table, (((1,), (1,)), ((), ())), preferred_element_type=jnp.float32
        )

    return lax.fori_loop(0, length // block_width, fold_one_block, running)


def build_table(targets, sources):
    source_count = sources.shape[1]
    block_width = math.gcd(source_count, 1024)
    table = jnp.zeros((targets.shape[1], source_count), jnp.bfloat16)

    def build_one_block(number, filled):
        inside = number * block_width
        part_points = lax.dynamic_slice_in_dim(sources, inside, block_width, 1)
        return lax.dynamic_update_slice_in_dim(
            filled, single_layer(targets, part_points), inside, 1
        )

    return lax.fori_loop(0, source_count // block_width, build_one_block, table)


def shared_shards(points, density, incident, precond, receivers):
    count_tgt = lax.axis_size("tgt")
    count_src = lax.axis_size("src")
    count_sub = lax.axis_size("sub")
    point_count = points.shape[1] * count_tgt * count_src * count_sub
    cell_area = FOUR_PI / point_count
    row_points = lax.all_gather(points, "src", axis=1, tiled=True)
    column_points = lax.all_gather(points, ("tgt", "sub"), axis=1, tiled=True)
    columns_count = density.shape[0]
    stored_table = build_table(row_points, column_points)
    for iteration in range(ITERS):
        weighted = (density * cell_area).astype(jnp.bfloat16)
        partial_sum = lax.dot_general(
            lax.all_gather(weighted, ("tgt", "sub"), axis=1, tiled=True),
            stored_table,
            (((1,), (1,)), ((), ())),
            preferred_element_type=jnp.float32,
        )
        field = lax.psum_scatter(partial_sum, "src", scatter_dimension=1, tiled=True)
        density = density - (field + incident) / precond[None, :]
    weighted = (density * cell_area).astype(jnp.bfloat16)
    receiver_blocks = receivers.reshape(count_tgt, count_src, count_sub, -1)
    picked = lax.dynamic_index_in_dim(receiver_blocks, lax.axis_index("tgt"), 0, keepdims=False)
    picked = lax.dynamic_index_in_dim(picked, lax.axis_index("sub"), 1, keepdims=False)
    toward = receiver_directions(picked.reshape(-1))
    empty_far = jnp.zeros((columns_count, toward.shape[1]), jnp.float32)
    far_partial = fold_blocks(
        empty_far,
        lax.all_gather(weighted, ("tgt", "sub"), axis=1, tiled=True),
        column_points,
        toward,
        far_kernel,
    )
    far_field = lax.psum_scatter(far_partial, "src", scatter_dimension=1, tiled=True)
    return (density, far_field)


def can_replicate(mesh, points):
    sizes = mesh.shape
    chips = sizes["tgt"] * sizes["src"]
    per_group = chips * sizes["sub"]
    total = points.shape[1] // sizes["groups"]
    return (
        sizes["sub"] == 2
        and chips >= 2
        and chips & (chips - 1) == 0
        and total == per_group * (BLOCK // 2)
        and total * total <= TABLE_LIMIT
    )


def solution(mesh):
    placed = (
        P(None, ("groups", "tgt", "src", "sub")),
        P(None, ("groups", "tgt", "src", "sub")),
        P(None, ("groups", "tgt", "src", "sub")),
        P(("groups", "tgt", "src", "sub")),
        P("groups"),
    )

    def whole(points, density, incident, precond, receivers):
        body = replicated_shards if can_replicate(mesh, points) else shared_shards
        return jax.shard_map(
            body,
            mesh=mesh,
            in_specs=placed,
            out_specs=(
                P(None, ("groups", "tgt", "src", "sub")),
                P(None, ("groups", "tgt", "src", "sub")),
            ),
            check_vma=False,
        )(points, density, incident, precond, receivers)

    return whole
```

```python
import math

import jax
import jax.numpy as jnp
from jax import lax
from jax.experimental import pallas as pl
from jax.experimental.pallas import tpu as pltpu
from jax.sharding import PartitionSpec as P

ITERS = 4
NDIR = 65536


WAVENUMBER = 32.0
SMOOTHING = 0.02
FOUR_PI = 4.0 * math.pi

TURNS = WAVENUMBER / (2.0 * math.pi)
SMOOTH_TURNS = (SMOOTHING * TURNS) ** 2
BLOCK = 256
TABLE_LIMIT = 8 * 2**20
VMEM_LIMIT = 24 * 2**20


def sine_coefficients(count):
    nodes = [0.03125 + 0.03125 * math.cos(math.pi * (k + 0.5) / count) for k in range(count)]
    values = [math.sin(2.0 * math.pi * math.sqrt(u)) / math.sqrt(u) for u in nodes]
    divided = list(values)
    for level in range(1, count):
        for k in range(count - 1, level - 1, -1):
            divided[k] = (divided[k] - divided[k - 1]) / (nodes[k] - nodes[k - level])
    poly = [0.0] * count
    for k in range(count - 1, -1, -1):
        shifted = [0.0] + poly[:-1]
        poly = [s - nodes[k] * p for s, p in zip(shifted, poly)]
        poly[0] += divided[k]
    return poly


SINE = sine_coefficients(4)


def cos_turns(turns, scale):
    folded = 0.25 - jnp.abs(turns - jnp.round(turns))
    square = folded * folded
    value = SINE[-1] * scale
    for c in SINE[-2::-1]:
        value = value * square + c * scale
    return value * folded


def green(squared):
    kept = jnp.maximum(squared, 1e-12)
    turns = kept * lax.rsqrt(kept)
    return (cos_turns(turns, TURNS / FOUR_PI) * lax.rsqrt(squared + SMOOTH_TURNS)).astype(jnp.bfloat16)


def split3(x):
    high = x.astype(jnp.bfloat16).astype(jnp.float32)
    rest = x - high
    mid = rest.astype(jnp.bfloat16).astype(jnp.float32)
    low = (rest - mid).astype(jnp.bfloat16).astype(jnp.float32)
    return high, mid, low


def pack_kernel(points, precond, density, incident, out, head, sems):
    columns = density.shape[0]
    moves = [
        (points, head.at[0]),
        (precond, head.at[1, pl.ds(0, 1)]),
        (density, out.at[pl.ds(8, columns)]),
        (incident, out.at[pl.ds(8 + columns, columns)]),
    ]
    copies = [pltpu.make_async_copy(src, dst, sems.at[k]) for k, (src, dst) in enumerate(moves)]
    for copy in copies:
        copy.start()
    copies[0].wait()
    copies[1].wait()
    out[0:3, :] = head[0]
    out[3:4, :] = head[1, 0:1]
    out[4:8, :] = jnp.zeros((4, out.shape[1]), jnp.float32)
    copies[2].wait()
    copies[3].wait()


def replicated_kernel(blocks, columns, *refs):
    data = refs[:blocks]
    toward_ref = refs[blocks]
    density_out, far_out = refs[blocks + 1 : blocks + 3]
    lhs, rhs, coords, table, half_table, plane, dens, inc = refs[blocks + 3 : blocks + 11]
    stage = refs[blocks + 11 :]
    total = blocks * BLOCK
    shards_per_block = data[0].shape[0]
    width = data[0].shape[2]
    full = blocks // 2

    def lanes(start, count):
        return jnp.concatenate(
            [data[b][s, start : start + count, :] for b in range(blocks) for s in range(shards_per_block)], axis=1
        )

    head = lanes(0, 8)
    scaled = head[0:3] * TURNS
    coords[0:3, :] = scaled
    inverse = 1.0 / head[3:4]
    dens[...] = lanes(8, columns)
    inc[...] = lanes(8 + columns, columns)

    ones = jnp.ones((1, total), jnp.float32)
    left, right = [], []
    for k in range(3):
        h, m, l = split3(scaled[k : k + 1])
        left += [-2.0 * h, -2.0 * h, -2.0 * m, -2.0 * m, -2.0 * h, -2.0 * l]
        right += [h, m, h, m, l, h]
    norm = scaled[0:1] * scaled[0:1] + scaled[1:2] * scaled[1:2] + scaled[2:3] * scaled[2:3]
    h, m, l = split3(norm)
    left += [h, m, l, ones, ones, ones]
    right += [ones, ones, ones, h, m, l]
    zeros = jnp.zeros((8, total), jnp.float32)
    left = jnp.concatenate(left + [zeros], axis=0)
    rhs[...] = jnp.concatenate(right + [zeros], axis=0).astype(jnp.bfloat16)
    lhs[...] = left.T.astype(jnp.bfloat16)

    def distances(row, count, column):
        return lax.dot_general(
            lhs[pl.ds(pl.multiple_of(row, 128), count), :],
            rhs[:, pl.ds(pl.multiple_of(column, BLOCK), BLOCK)],
            (((1,), (0,)), ((), ())),
            preferred_element_type=jnp.float32,
        )

    def fill(block, d, source):
        for r in range(0, BLOCK, 32):
            table[block, d, r : r + 32, :] = green(source[r : r + 32, :])

    stage[0][...] = distances(0, BLOCK, 0)

    def one_row(block, carry):
        for d in range(1, full):
            stage[d][...] = distances(block * BLOCK, BLOCK, lax.rem(block + d, blocks) * BLOCK)
            fill(block, d - 1, stage[d - 1])
        low = lax.rem(block, full)
        part = block // full
        stage[full][...] = distances(low * BLOCK + part * 128, 128, (low + full) * BLOCK)
        fill(block, full - 1, stage[full - 1])
        following = lax.rem(block + 1, blocks) * BLOCK
        stage[0][...] = distances(following, BLOCK, following)
        base = pl.multiple_of(part * 128, 128)
        for r in range(0, 128, 32):
            half_table[low, pl.ds(base + r, 32), :] = green(stage[full][r : r + 32, :])
        return carry

    lax.fori_loop(0, blocks, one_row, 0)

    toward = toward_ref[...].T
    cell_area = FOUR_PI / total

    def rounded():
        return (dens[...] * cell_area).astype(jnp.bfloat16)

    def part_of(w, b):
        b = b % blocks
        return w[:, b * BLOCK : (b + 1) * BLOCK]

    def entry(b, d):
        b = b % blocks
        return table[b, d] if d < full else half_table[b]

    def down(w, kernel_block):
        return lax.dot_general(w, kernel_block, (((1,), (0,)), ((), ())), preferred_element_type=jnp.float32)

    def across(kernel_block, w):
        return lax.dot_general(kernel_block, w, (((1,), (1,)), ((), ())), preferred_element_type=jnp.float32)

    per_step = -(-blocks // ITERS)

    def iterate(step, carry):
        w = rounded()
        for k in range(per_step):
            b = jnp.minimum(step * per_step + k, blocks - 1)
            span = pl.ds(pl.multiple_of(b * BLOCK, BLOCK), BLOCK)
            phase = toward[:, 0:1] * coords[0:1, span] + toward[:, 1:2] * coords[1:2, span]
            phase = phase + toward[:, 2:3] * coords[2:3, span]
            plane[:, span] = cos_turns(phase, 1.0).astype(jnp.bfloat16)
        for b in range(blocks):
            field = down(part_of(w, b), entry(b, 0))
            turned = None
            for d in range(1, full + 1):
                if d < full or b >= full:
                    field += down(part_of(w, b - d), entry(b - d, d))
                if d < full or b < full:
                    term = across(entry(b, d), part_of(w, b + d))
                    turned = term if turned is None else turned + term
            field += turned.T
            span = slice(b * BLOCK, (b + 1) * BLOCK)
            dens[:, span] = dens[:, span] - (field + inc[:, span]) * inverse[:, span]
        return carry

    lax.fori_loop(0, ITERS, iterate, 0)
    density_out[...] = dens[:, 0:width]
    far_out[...] = across(plane[...], rounded()).T


def replicated_shards(points, density, incident, precond, receivers):
    count_tgt = lax.axis_size("tgt")
    count_src = lax.axis_size("src")
    count_sub = lax.axis_size("sub")
    chips = count_tgt * count_src
    columns, width = density.shape
    names = ("tgt", "src", "sub")
    vmem = pl.BlockSpec(memory_space=pltpu.VMEM)
    payload = pl.pallas_call(
        pack_kernel,
        out_shape=jax.ShapeDtypeStruct((8 + 2 * columns, width), jnp.float32),
        in_specs=[pl.BlockSpec(memory_space=pltpu.HBM)] * 4,
        out_specs=vmem,
        scratch_shapes=[pltpu.VMEM((2, 3, width), jnp.float32), pltpu.SemaphoreType.DMA((4,))],
        compiler_params=pltpu.CompilerParams(vmem_limit_bytes=4 * 2**20),
        name="pack",
    )(*(pltpu.with_memory_space_constraint(a, pltpu.HBM) for a in (points, precond[None, :], density, incident)))
    swap = [(0, 1), (1, 0)]
    own = jnp.stack([payload, lax.ppermute(payload, "sub", swap)])

    def fetch(offsets):
        pairs = [(q * 2 + c, (q ^ offsets[c]) * 2 + c) for q in range(chips) for c in range(2)]
        return lax.ppermute(own, names, pairs)

    held = [own]
    for k in range(1, chips - 1, 2):
        near = fetch((k, k + 1))
        held += [near, lax.ppermute(near, "sub", swap)]
    held.append(fetch((chips - 1, chips - 1)))

    place = (lax.axis_index("tgt") * count_src + lax.axis_index("src")) * count_sub + lax.axis_index("sub")
    rows = receivers.shape[0] // (chips * count_sub)
    toward = receiver_directions(lax.dynamic_slice_in_dim(receivers, place * rows, rows, 0))
    toward = jnp.concatenate([toward, jnp.zeros((5, rows), jnp.float32)], axis=0)

    blocks = len(held)
    total = blocks * BLOCK
    full = blocks // 2
    return pl.pallas_call(
        lambda *refs: replicated_kernel(blocks, columns, *refs),
        out_shape=(
            jax.ShapeDtypeStruct((columns, width), jnp.float32),
            jax.ShapeDtypeStruct((columns, rows), jnp.float32),
        ),
        in_specs=[vmem] * (blocks + 1),
        out_specs=(vmem, vmem),
        scratch_shapes=[
            pltpu.VMEM((total, 32), jnp.bfloat16),
            pltpu.VMEM((32, total), jnp.bfloat16),
            pltpu.VMEM((8, total), jnp.float32),
            pltpu.VMEM((blocks, full, BLOCK, BLOCK), jnp.bfloat16),
            pltpu.VMEM((full, BLOCK, BLOCK), jnp.bfloat16),
            pltpu.VMEM((rows, total), jnp.bfloat16),
            pltpu.VMEM((columns, total), jnp.float32),
            pltpu.VMEM((columns, total), jnp.float32),
        ]
        + [pltpu.VMEM((BLOCK, BLOCK), jnp.float32) for _ in range(full)]
        + [pltpu.VMEM((128, BLOCK), jnp.float32)],
        compiler_params=pltpu.CompilerParams(vmem_limit_bytes=VMEM_LIMIT),
        name="iterate",
    )(*held, toward)


def single_layer(targets, sources):
    delta_x = targets[0][:, None] - sources[0][None, :]
    delta_y = targets[1][:, None] - sources[1][None, :]
    delta_z = targets[2][:, None] - sources[2][None, :]
    squared = delta_x * delta_x + delta_y * delta_y + delta_z * delta_z
    values = jnp.cos(WAVENUMBER * jnp.sqrt(squared)) / (
        FOUR_PI * jnp.sqrt(squared + SMOOTHING * SMOOTHING)
    )
    return values.astype(jnp.bfloat16)


def far_kernel(toward, sources):
    projection = toward[0][:, None] * sources[0][None, :] + toward[1][:, None] * sources[1][None, :]
    projection = projection + toward[2][:, None] * sources[2][None, :]
    return jnp.cos(WAVENUMBER * projection).astype(jnp.bfloat16)


def receiver_directions(direction_index):
    upper_part = direction_index // 256
    lower_part = direction_index % 256
    rotation = (upper_part * 14080 + lower_part * 40503) % 65536
    azimuth = rotation.astype(jnp.float32) * (2.0 * math.pi / 65536.0)
    height = 1.0 - (2 * direction_index + 1).astype(jnp.float32) / NDIR
    radial = jnp.sqrt(jnp.maximum(1.0 - height * height, 0.0))
    return jnp.stack([radial * jnp.cos(azimuth), radial * jnp.sin(azimuth), height])


def fold_blocks(running, incoming, coordinates, targets, maker):
    length = incoming.shape[1]
    block_width = math.gcd(length, 1024)

    def fold_one_block(number, accumulated):
        inside = number * block_width
        part_density = lax.dynamic_slice_in_dim(incoming, inside, block_width, 1)
        part_points = lax.dynamic_slice_in_dim(coordinates, inside, block_width, 1)
        kernel_table = maker(targets, part_points)
        return accumulated + lax.dot_general(
            part_density, kernel_table, (((1,), (1,)), ((), ())), preferred_element_type=jnp.float32
        )

    return lax.fori_loop(0, length // block_width, fold_one_block, running)


def build_table(targets, sources):
    source_count = sources.shape[1]
    block_width = math.gcd(source_count, 1024)
    table = jnp.zeros((targets.shape[1], source_count), jnp.bfloat16)

    def build_one_block(number, filled):
        inside = number * block_width
        part_points = lax.dynamic_slice_in_dim(sources, inside, block_width, 1)
        return lax.dynamic_update_slice_in_dim(
            filled, single_layer(targets, part_points), inside, 1
        )

    return lax.fori_loop(0, source_count // block_width, build_one_block, table)


def shared_shards(points, density, incident, precond, receivers):
    count_tgt = lax.axis_size("tgt")
    count_src = lax.axis_size("src")
    count_sub = lax.axis_size("sub")
    point_count = points.shape[1] * count_tgt * count_src * count_sub
    cell_area = FOUR_PI / point_count
    row_points = lax.all_gather(points, "src", axis=1, tiled=True)
    column_points = lax.all_gather(points, ("tgt", "sub"), axis=1, tiled=True)
    columns_count = density.shape[0]
    stored_table = build_table(row_points, column_points)
    for iteration in range(ITERS):
        weighted = (density * cell_area).astype(jnp.bfloat16)
        partial_sum = lax.dot_general(
            lax.all_gather(weighted, ("tgt", "sub"), axis=1, tiled=True),
            stored_table,
            (((1,), (1,)), ((), ())),
            preferred_element_type=jnp.float32,
        )
        field = lax.psum_scatter(partial_sum, "src", scatter_dimension=1, tiled=True)
        density = density - (field + incident) / precond[None, :]
    weighted = (density * cell_area).astype(jnp.bfloat16)
    receiver_blocks = receivers.reshape(count_tgt, count_src, count_sub, -1)
    picked = lax.dynamic_index_in_dim(receiver_blocks, lax.axis_index("tgt"), 0, keepdims=False)
    picked = lax.dynamic_index_in_dim(picked, lax.axis_index("sub"), 1, keepdims=False)
    toward = receiver_directions(picked.reshape(-1))
    empty_far = jnp.zeros((columns_count, toward.shape[1]), jnp.float32)
    far_partial = fold_blocks(
        empty_far,
        lax.all_gather(weighted, ("tgt", "sub"), axis=1, tiled=True),
        column_points,
        toward,
        far_kernel,
    )
    far_field = lax.psum_scatter(far_partial, "src", scatter_dimension=1, tiled=True)
    return (density, far_field)


def can_replicate(mesh, points):
    sizes = mesh.shape
    chips = sizes["tgt"] * sizes["src"]
    per_group = chips * sizes["sub"]
    total = points.shape[1] // sizes["groups"]
    return (
        sizes["sub"] == 2
        and chips >= 4
        and chips & (chips - 1) == 0
        and total == per_group * (BLOCK // 2)
        and total * total <= TABLE_LIMIT
    )


def solution(mesh):
    placed = (
        P(None, ("groups", "tgt", "src", "sub")),
        P(None, ("groups", "tgt", "src", "sub")),
        P(None, ("groups", "tgt", "src", "sub")),
        P(("groups", "tgt", "src", "sub")),
        P("groups"),
    )

    def whole(points, density, incident, precond, receivers):
        body = replicated_shards if can_replicate(mesh, points) else shared_shards
        return jax.shard_map(
            body,
            mesh=mesh,
            in_specs=placed,
            out_specs=(
                P(None, ("groups", "tgt", "src", "sub")),
                P(None, ("groups", "tgt", "src", "sub")),
            ),
            check_vma=False,
        )(points, density, incident, precond, receivers)

    return whole
```

```python
import functools
import math

import jax
import jax.numpy as jnp
from jax import lax
from jax.experimental import pallas as pl
from jax.experimental.pallas import tpu as pltpu
from jax.sharding import PartitionSpec as P

ITERS = 4
NDIR = 65536


WAVENUMBER = 32.0
SMOOTHING = 0.02
FOUR_PI = 4.0 * math.pi

TURNS = WAVENUMBER / (2.0 * math.pi)
SMOOTH_TURNS = (SMOOTHING * TURNS) ** 2
BLOCK = 256
TABLE_LIMIT = 8 * 2**20
VMEM_LIMIT = 24 * 2**20


def sine_coefficients(count):
    nodes = [0.03125 + 0.03125 * math.cos(math.pi * (k + 0.5) / count) for k in range(count)]
    values = [math.sin(2.0 * math.pi * math.sqrt(u)) / math.sqrt(u) for u in nodes]
    divided = list(values)
    for level in range(1, count):
        for k in range(count - 1, level - 1, -1):
            divided[k] = (divided[k] - divided[k - 1]) / (nodes[k] - nodes[k - level])
    poly = [0.0] * count
    for k in range(count - 1, -1, -1):
        shifted = [0.0] + poly[:-1]
        poly = [s - nodes[k] * p for s, p in zip(shifted, poly)]
        poly[0] += divided[k]
    return poly


SINE = sine_coefficients(4)


def cos_turns(turns, scale):
    folded = 0.25 - jnp.abs(turns - jnp.round(turns))
    square = folded * folded
    value = SINE[-1] * scale
    for c in SINE[-2::-1]:
        value = value * square + c * scale
    return value * folded


def green(squared):
    kept = jnp.maximum(squared, 1e-12)
    turns = kept * lax.rsqrt(kept)
    return (cos_turns(turns, TURNS / FOUR_PI) * lax.rsqrt(squared + SMOOTH_TURNS)).astype(jnp.bfloat16)


def split3(x):
    high = x.astype(jnp.bfloat16).astype(jnp.float32)
    rest = x - high
    mid = rest.astype(jnp.bfloat16).astype(jnp.float32)
    low = (rest - mid).astype(jnp.bfloat16).astype(jnp.float32)
    return high, mid, low


def pack_kernel(points, precond, density, incident, out, head, sems):
    columns = density.shape[0]
    moves = [
        (points, head.at[0]),
        (precond, head.at[1, pl.ds(0, 1)]),
        (density, out.at[pl.ds(8, columns)]),
        (incident, out.at[pl.ds(8 + columns, columns)]),
    ]
    copies = [pltpu.make_async_copy(src, dst, sems.at[k]) for k, (src, dst) in enumerate(moves)]
    for copy in copies:
        copy.start()
    copies[0].wait()
    copies[1].wait()
    out[0:3, :] = head[0]
    out[3:4, :] = head[1, 0:1]
    out[4:8, :] = jnp.zeros((4, out.shape[1]), jnp.float32)
    copies[2].wait()
    copies[3].wait()


def lanes(data, start, count):
    return jnp.concatenate(
        [piece[s, start : start + count, :] for piece in data for s in range(piece.shape[0])], axis=1
    )


def distance_operands(scaled):
    ones = jnp.ones((1, scaled.shape[1]), jnp.float32)
    left, right = [], []
    for k in range(3):
        h, m, l = split3(scaled[k : k + 1])
        left += [-2.0 * h, -2.0 * h, -2.0 * m, -2.0 * m, -2.0 * h, -2.0 * l]
        right += [h, m, h, m, l, h]
    norm = scaled[0:1] * scaled[0:1] + scaled[1:2] * scaled[1:2] + scaled[2:3] * scaled[2:3]
    h, m, l = split3(norm)
    left += [h, m, l, ones, ones, ones]
    right += [ones, ones, ones, h, m, l]
    zeros = jnp.zeros((8, scaled.shape[1]), jnp.float32)
    left = jnp.concatenate(left + [zeros], axis=0)
    right = jnp.concatenate(right + [zeros], axis=0).astype(jnp.bfloat16)
    return left.T.astype(jnp.bfloat16), right


def down(w, kernel_block):
    return lax.dot_general(w, kernel_block, (((1,), (0,)), ((), ())), preferred_element_type=jnp.float32)


def across(kernel_block, w):
    return lax.dot_general(kernel_block, w, (((1,), (1,)), ((), ())), preferred_element_type=jnp.float32)


def block_span(index):
    return pl.ds(pl.multiple_of(index * BLOCK, BLOCK), BLOCK)


def strip_size(old, new):
    return sum(j + 1 for j in range(old, old + new))


def build_strips(old, new, lhs, rhs, weighted, table, field, turned, even, odd):
    count = strip_size(old, new)
    starts = [strip_size(old, k) for k in range(new)]

    def place(k):
        j, i = 0, k
        for step in range(1, new):
            past = k >= starts[step]
            j = jnp.where(past, step, j)
            i = jnp.where(past, k - starts[step], i)
        return j, i

    def distances(k):
        j, i = place(k)
        return lax.dot_general(
            lhs[block_span(j), :], rhs[:, block_span(i)], (((1,), (0,)), ((), ())), preferred_element_type=jnp.float32
        )

    def fill(k, source):
        for r in range(0, BLOCK, 32):
            table[k, r : r + 32, :] = green(source[r : r + 32, :])

    def products(k, valid):
        j, i = place(k)
        valid = jnp.where(valid, 1.0, 0.0)
        beside = jnp.where(old + j == i, 0.0, valid).astype(jnp.bfloat16)
        row = block_span(j)
        turned[row, :] += across(table[k], weighted[:, block_span(i)] * valid.astype(jnp.bfloat16))
        field[:, block_span(i)] += down(weighted[:, block_span(old + j)] * beside, table[k])

    field[...] = jnp.zeros_like(field)
    turned[...] = jnp.zeros_like(turned)
    table[0] = jnp.zeros((BLOCK, BLOCK), jnp.bfloat16)
    even[...] = distances(0)

    def pair(t, carry):
        k = 2 * t
        odd[...] = distances(k + 1)
        products(jnp.maximum(k - 1, 0), k > 0)
        fill(k, even)
        even[...] = distances(jnp.minimum(k + 2, count - 1))
        products(k, True)
        fill(k + 1, odd)
        return carry

    lax.fori_loop(0, count // 2, pair, 0)
    if count >= 2:
        products(2 * (count // 2) - 1, True)
    if count % 2:
        fill(count - 1, even)
        products(count - 1, True)
    field[:, old * BLOCK :] += turned[...].T


def prepare(old, data, columns, total, lhs, rhs, weighted, before):
    scaled = lanes(data, 0, 3) * TURNS
    left, right = distance_operands(scaled)
    lhs[...] = left
    rhs[:, old * BLOCK :] = right
    weighted[:, old * BLOCK :] = (lanes(data, 8, columns) * (FOUR_PI / total)).astype(jnp.bfloat16)
    if old:
        rhs[:, : old * BLOCK] = before[0][...]
        weighted[:, : old * BLOCK] = before[1][...]
    return scaled


def strips_kernel(pieces, old, new, columns, total, *refs):
    data, refs = refs[:pieces], refs[pieces:]
    before = refs[: 2 if old else 0]
    table, field, rhs, weighted, lhs, turned, even, odd = refs[len(before) :]
    prepare(old, data, columns, total, lhs, rhs, weighted, before)
    build_strips(old, new, lhs, rhs, weighted, table, field, turned, even, odd)


def iterate_kernel(pieces, blocks, columns, groups, *refs):
    data, refs = refs[:pieces], refs[pieces:]
    last, toward_ref, before, refs = refs[0], refs[1], refs[2:4], refs[4:]
    tables, refs = refs[: len(groups)], refs[len(groups) :]
    fields, refs = refs[: len(groups)], refs[len(groups) :]
    density_out, far_out = refs[:2]
    lhs, rhs, weighted, table, field, turned, even, odd, coords, plane, dens, inc = refs[2:]
    total = blocks * BLOCK
    width = data[0].shape[2]
    old = blocks - 1
    prepare(old, [last], columns, total, lhs, rhs, weighted, before)
    build_strips(old, 1, lhs, rhs, weighted, table, field, turned, even, odd)

    everything = list(data) + [last]
    coords[0:3, :] = lanes(everything, 0, 3) * TURNS
    inverse = 1.0 / lanes(everything, 3, 1)
    dens[...] = lanes(everything, 8, columns)
    inc[...] = lanes(everything, 8 + columns, columns)
    for part in fields:
        field[:, : part.shape[1]] += part[...]
    dens[...] = dens[...] - (field[...] + inc[...]) * inverse

    entries = {}
    for (first, count), part in zip(list(groups) + [(old, 1)], list(tables) + [table]):
        k = 0
        for j in range(first, first + count):
            for i in range(j + 1):
                entries[j, i] = (part, k)
                k += 1

    def entry(j, i):
        part, k = entries[j, i]
        return part[k]

    toward = toward_ref[...].T
    cell_area = FOUR_PI / total

    def rounded():
        return (dens[...] * cell_area).astype(jnp.bfloat16)

    def part_of(w, b):
        return w[:, b * BLOCK : (b + 1) * BLOCK]

    steps = ITERS - 1
    per_step = -(-blocks // steps)

    def iterate(step, carry):
        w = rounded()
        for k in range(per_step):
            span = block_span(jnp.minimum(step * per_step + k, blocks - 1))
            phase = toward[:, 0:1] * coords[0:1, span] + toward[:, 1:2] * coords[1:2, span]
            phase = phase + toward[:, 2:3] * coords[2:3, span]
            plane[:, span] = cos_turns(phase, 1.0).astype(jnp.bfloat16)
        for b in range(blocks):
            total_field = None
            for j in range(b, blocks):
                term = down(part_of(w, j), entry(j, b))
                total_field = term if total_field is None else total_field + term
            side = None
            for i in range(b):
                term = across(entry(b, i), part_of(w, i))
                side = term if side is None else side + term
            if side is not None:
                total_field += side.T
            span = slice(b * BLOCK, (b + 1) * BLOCK)
            dens[:, span] = dens[:, span] - (total_field + inc[:, span]) * inverse[:, span]
        return carry

    lax.fori_loop(0, steps, iterate, 0)
    density_out[...] = dens[:, 0:width]
    far_out[...] = across(plane[...], rounded()).T


def replicated_shards(points, density, incident, precond, receivers):
    count_tgt = lax.axis_size("tgt")
    count_src = lax.axis_size("src")
    count_sub = lax.axis_size("sub")
    chips = count_tgt * count_src
    columns, width = density.shape
    names = ("tgt", "src", "sub")
    vmem = pl.BlockSpec(memory_space=pltpu.VMEM)
    payload = pl.pallas_call(
        pack_kernel,
        out_shape=jax.ShapeDtypeStruct((8 + 2 * columns, width), jnp.float32),
        in_specs=[pl.BlockSpec(memory_space=pltpu.HBM)] * 4,
        out_specs=vmem,
        scratch_shapes=[pltpu.VMEM((2, 3, width), jnp.float32), pltpu.SemaphoreType.DMA((4,))],
        compiler_params=pltpu.CompilerParams(vmem_limit_bytes=4 * 2**20),
        name="pack",
    )(*(pltpu.with_memory_space_constraint(a, pltpu.HBM) for a in (points, precond[None, :], density, incident)))
    swap = [(0, 1), (1, 0)]
    payload = payload[None]

    def fetch(array, offsets):
        pairs = [(q * 2 + c, (q ^ offsets[c]) * 2 + c) for q in range(chips) for c in range(2)]
        return lax.ppermute(array, names, pairs)

    own = jnp.concatenate([payload, lax.ppermute(payload, "sub", swap)], axis=0)
    near = [fetch(own, (k, k + 1)) for k in range(1, chips - 1, 2)]
    last = fetch(own, (chips - 1, chips - 1))

    place = (lax.axis_index("tgt") * count_src + lax.axis_index("src")) * count_sub + lax.axis_index("sub")
    rows = receivers.shape[0] // (chips * count_sub)
    toward = receiver_directions(lax.dynamic_slice_in_dim(receivers, place * rows, rows, 0))
    toward = jnp.concatenate([toward, jnp.zeros((5, rows), jnp.float32)], axis=0)

    blocks = chips
    total = blocks * BLOCK
    f32, bf16 = jnp.float32, jnp.bfloat16

    def strip_shapes(old, new):
        return [
            ((strip_size(old, new), BLOCK, BLOCK), bf16),
            ((columns, (old + new) * BLOCK), f32),
            ((32, (old + new) * BLOCK), bf16),
            ((columns, (old + new) * BLOCK), bf16),
            ((new * BLOCK, 32), bf16),
            ((new * BLOCK, columns), f32),
            ((BLOCK, BLOCK), f32),
            ((BLOCK, BLOCK), f32),
        ]

    groups, tables, fields, held, before = [], [], [], [], []

    def strips(data):
        old, new = len(held), len(data)
        shapes = strip_shapes(old, new)
        work = strip_size(old, new) * BLOCK * BLOCK
        table, field, *state = pl.pallas_call(
            functools.partial(strips_kernel, new, old, new, columns, total),
            out_shape=[jax.ShapeDtypeStruct(*shape) for shape in shapes[:4]],
            in_specs=[vmem] * (new + len(before)),
            out_specs=[vmem] * 4,
            scratch_shapes=[pltpu.VMEM(*shape) for shape in shapes[4:]],
            compiler_params=pltpu.CompilerParams(vmem_limit_bytes=VMEM_LIMIT),
            cost_estimate=pl.CostEstimate(flops=30 * work, bytes_accessed=2 * work, transcendentals=2 * work),
            name=f"strips{old}",
        )(*data, *before)
        groups.append((old, new))
        tables.append(table)
        fields.append(field)
        held.extend(data)
        before[:] = state

    early, late = near[:2], near[2:]
    swapped = [lax.ppermute(array, "sub", swap) for array in early]
    strips([own, early[0], swapped[0]])
    for array, other in zip(early[1:], swapped[1:]):
        strips([array, other])
    for array in late:
        array, fields[-1] = lax.optimization_barrier((array, fields[-1]))
        other = lax.ppermute(array, "sub", swap)
        strips([array])
        strips([other])

    old = len(held)
    pieces = len(held)
    shapes = strip_shapes(old, 1)
    return pl.pallas_call(
        functools.partial(iterate_kernel, pieces, blocks, columns, tuple(groups)),
        out_shape=(
            jax.ShapeDtypeStruct((columns, width), f32),
            jax.ShapeDtypeStruct((columns, rows), f32),
        ),
        in_specs=[vmem] * (pieces + 4 + 2 * len(groups)),
        out_specs=(vmem, vmem),
        scratch_shapes=[pltpu.VMEM(*shapes[k]) for k in (4, 2, 3, 0, 1, 5, 6, 7)]
        + [
            pltpu.VMEM((8, total), f32),
            pltpu.VMEM((rows, total), bf16),
            pltpu.VMEM((columns, total), f32),
            pltpu.VMEM((columns, total), f32),
        ],
        compiler_params=pltpu.CompilerParams(vmem_limit_bytes=VMEM_LIMIT),
        name="iterate",
    )(*held, last, toward, *before, *tables, *fields)


def single_layer(targets, sources):
    delta_x = targets[0][:, None] - sources[0][None, :]
    delta_y = targets[1][:, None] - sources[1][None, :]
    delta_z = targets[2][:, None] - sources[2][None, :]
    squared = delta_x * delta_x + delta_y * delta_y + delta_z * delta_z
    values = jnp.cos(WAVENUMBER * jnp.sqrt(squared)) / (
        FOUR_PI * jnp.sqrt(squared + SMOOTHING * SMOOTHING)
    )
    return values.astype(jnp.bfloat16)


def far_kernel(toward, sources):
    projection = toward[0][:, None] * sources[0][None, :] + toward[1][:, None] * sources[1][None, :]
    projection = projection + toward[2][:, None] * sources[2][None, :]
    return jnp.cos(WAVENUMBER * projection).astype(jnp.bfloat16)


def receiver_directions(direction_index):
    upper_part = direction_index // 256
    lower_part = direction_index % 256
    rotation = (upper_part * 14080 + lower_part * 40503) % 65536
    azimuth = rotation.astype(jnp.float32) * (2.0 * math.pi / 65536.0)
    height = 1.0 - (2 * direction_index + 1).astype(jnp.float32) / NDIR
    radial = jnp.sqrt(jnp.maximum(1.0 - height * height, 0.0))
    return jnp.stack([radial * jnp.cos(azimuth), radial * jnp.sin(azimuth), height])


def fold_blocks(running, incoming, coordinates, targets, maker):
    length = incoming.shape[1]
    block_width = math.gcd(length, 1024)

    def fold_one_block(number, accumulated):
        inside = number * block_width
        part_density = lax.dynamic_slice_in_dim(incoming, inside, block_width, 1)
        part_points = lax.dynamic_slice_in_dim(coordinates, inside, block_width, 1)
        kernel_table = maker(targets, part_points)
        return accumulated + lax.dot_general(
            part_density, kernel_table, (((1,), (1,)), ((), ())), preferred_element_type=jnp.float32
        )

    return lax.fori_loop(0, length // block_width, fold_one_block, running)


def build_table(targets, sources):
    source_count = sources.shape[1]
    block_width = math.gcd(source_count, 1024)
    table = jnp.zeros((targets.shape[1], source_count), jnp.bfloat16)

    def build_one_block(number, filled):
        inside = number * block_width
        part_points = lax.dynamic_slice_in_dim(sources, inside, block_width, 1)
        return lax.dynamic_update_slice_in_dim(
            filled, single_layer(targets, part_points), inside, 1
        )

    return lax.fori_loop(0, source_count // block_width, build_one_block, table)


def shared_shards(points, density, incident, precond, receivers):
    count_tgt = lax.axis_size("tgt")
    count_src = lax.axis_size("src")
    count_sub = lax.axis_size("sub")
    point_count = points.shape[1] * count_tgt * count_src * count_sub
    cell_area = FOUR_PI / point_count
    row_points = lax.all_gather(points, "src", axis=1, tiled=True)
    column_points = lax.all_gather(points, ("tgt", "sub"), axis=1, tiled=True)
    columns_count = density.shape[0]
    stored_table = build_table(row_points, column_points)
    for iteration in range(ITERS):
        weighted = (density * cell_area).astype(jnp.bfloat16)
        partial_sum = lax.dot_general(
            lax.all_gather(weighted, ("tgt", "sub"), axis=1, tiled=True),
            stored_table,
            (((1,), (1,)), ((), ())),
            preferred_element_type=jnp.float32,
        )
        field = lax.psum_scatter(partial_sum, "src", scatter_dimension=1, tiled=True)
        density = density - (field + incident) / precond[None, :]
    weighted = (density * cell_area).astype(jnp.bfloat16)
    receiver_blocks = receivers.reshape(count_tgt, count_src, count_sub, -1)
    picked = lax.dynamic_index_in_dim(receiver_blocks, lax.axis_index("tgt"), 0, keepdims=False)
    picked = lax.dynamic_index_in_dim(picked, lax.axis_index("sub"), 1, keepdims=False)
    toward = receiver_directions(picked.reshape(-1))
    empty_far = jnp.zeros((columns_count, toward.shape[1]), jnp.float32)
    far_partial = fold_blocks(
        empty_far,
        lax.all_gather(weighted, ("tgt", "sub"), axis=1, tiled=True),
        column_points,
        toward,
        far_kernel,
    )
    far_field = lax.psum_scatter(far_partial, "src", scatter_dimension=1, tiled=True)
    return (density, far_field)


def can_replicate(mesh, points):
    sizes = mesh.shape
    chips = sizes["tgt"] * sizes["src"]
    per_group = chips * sizes["sub"]
    total = points.shape[1] // sizes["groups"]
    return (
        sizes["sub"] == 2
        and chips >= 4
        and chips & (chips - 1) == 0
        and total == per_group * (BLOCK // 2)
        and total * total <= TABLE_LIMIT
    )


def solution(mesh):
    placed = (
        P(None, ("groups", "tgt", "src", "sub")),
        P(None, ("groups", "tgt", "src", "sub")),
        P(None, ("groups", "tgt", "src", "sub")),
        P(("groups", "tgt", "src", "sub")),
        P("groups"),
    )

    def whole(points, density, incident, precond, receivers):
        body = replicated_shards if can_replicate(mesh, points) else shared_shards
        return jax.shard_map(
            body,
            mesh=mesh,
            in_specs=placed,
            out_specs=(
                P(None, ("groups", "tgt", "src", "sub")),
                P(None, ("groups", "tgt", "src", "sub")),
            ),
            check_vma=False,
        )(points, density, incident, precond, receivers)

    return whole
```

```python
import functools
import math

import jax
import jax.numpy as jnp
from jax import lax
from jax.experimental import pallas as pl
from jax.experimental.pallas import tpu as pltpu
from jax.sharding import PartitionSpec as P

ITERS = 4
NDIR = 65536


WAVENUMBER = 32.0
SMOOTHING = 0.02
FOUR_PI = 4.0 * math.pi

TURNS = WAVENUMBER / (2.0 * math.pi)
SMOOTH_TURNS = (SMOOTHING * TURNS) ** 2
BLOCK = 256
TABLE_LIMIT = 8 * 2**20
VMEM_LIMIT = 24 * 2**20


def sine_coefficients(count):
    nodes = [0.03125 + 0.03125 * math.cos(math.pi * (k + 0.5) / count) for k in range(count)]
    values = [math.sin(2.0 * math.pi * math.sqrt(u)) / math.sqrt(u) for u in nodes]
    divided = list(values)
    for level in range(1, count):
        for k in range(count - 1, level - 1, -1):
            divided[k] = (divided[k] - divided[k - 1]) / (nodes[k] - nodes[k - level])
    poly = [0.0] * count
    for k in range(count - 1, -1, -1):
        shifted = [0.0] + poly[:-1]
        poly = [s - nodes[k] * p for s, p in zip(shifted, poly)]
        poly[0] += divided[k]
    return poly


SINE = sine_coefficients(4)


def cos_turns(turns, scale):
    folded = 0.25 - jnp.abs(turns - jnp.round(turns))
    square = folded * folded
    value = SINE[-1] * scale
    for c in SINE[-2::-1]:
        value = value * square + c * scale
    return value * folded


def green(squared):
    kept = jnp.maximum(squared, 1e-12)
    turns = kept * lax.rsqrt(kept)
    return (cos_turns(turns, TURNS / FOUR_PI) * lax.rsqrt(squared + SMOOTH_TURNS)).astype(jnp.bfloat16)


def split3(x):
    high = x.astype(jnp.bfloat16).astype(jnp.float32)
    rest = x - high
    mid = rest.astype(jnp.bfloat16).astype(jnp.float32)
    low = (rest - mid).astype(jnp.bfloat16).astype(jnp.float32)
    return high, mid, low


def pack_kernel(points, precond, density, incident, out, head, sems):
    columns = density.shape[0]
    moves = [
        (points, head.at[0]),
        (precond, head.at[1, pl.ds(0, 1)]),
        (density, out.at[pl.ds(8, columns)]),
        (incident, out.at[pl.ds(8 + columns, columns)]),
    ]
    copies = [pltpu.make_async_copy(src, dst, sems.at[k]) for k, (src, dst) in enumerate(moves)]
    for copy in copies:
        copy.start()
    copies[0].wait()
    copies[1].wait()
    out[0:3, :] = head[0]
    out[3:4, :] = head[1, 0:1]
    out[4:8, :] = jnp.zeros((4, out.shape[1]), jnp.float32)
    copies[2].wait()
    copies[3].wait()


def lanes(data, start, count):
    return jnp.concatenate(
        [piece[s, start : start + count, :] for piece in data for s in range(piece.shape[0])], axis=1
    )


def distance_operands(scaled):
    ones = jnp.ones((1, scaled.shape[1]), jnp.float32)
    left, right = [], []
    for k in range(3):
        h, m, l = split3(scaled[k : k + 1])
        left += [-2.0 * h, -2.0 * h, -2.0 * m, -2.0 * m, -2.0 * h, -2.0 * l]
        right += [h, m, h, m, l, h]
    norm = scaled[0:1] * scaled[0:1] + scaled[1:2] * scaled[1:2] + scaled[2:3] * scaled[2:3]
    h, m, l = split3(norm)
    left += [h, m, l, ones, ones, ones]
    right += [ones, ones, ones, h, m, l]
    zeros = jnp.zeros((8, scaled.shape[1]), jnp.float32)
    left = jnp.concatenate(left + [zeros], axis=0)
    right = jnp.concatenate(right + [zeros], axis=0).astype(jnp.bfloat16)
    return left.T.astype(jnp.bfloat16), right


def down(w, kernel_block):
    return lax.dot_general(w, kernel_block, (((1,), (0,)), ((), ())), preferred_element_type=jnp.float32)


def across(kernel_block, w):
    return lax.dot_general(kernel_block, w, (((1,), (1,)), ((), ())), preferred_element_type=jnp.float32)


def block_span(index):
    return pl.ds(pl.multiple_of(index * BLOCK, BLOCK), BLOCK)


def strip_size(old, new):
    return sum(j + 1 for j in range(old, old + new))


def build_strips(old, new, lhs, rhs, weighted, table, field, turned, even, odd):
    count = strip_size(old, new)
    starts = [strip_size(old, k) for k in range(new)]

    def place(k):
        j, i = 0, k
        for step in range(1, new):
            past = k >= starts[step]
            j = jnp.where(past, step, j)
            i = jnp.where(past, k - starts[step], i)
        return j, i

    def distances(k):
        j, i = place(k)
        return lax.dot_general(
            lhs[block_span(j), :], rhs[:, block_span(i)], (((1,), (0,)), ((), ())), preferred_element_type=jnp.float32
        )

    def fill(k, source):
        for r in range(0, BLOCK, 32):
            table[k, r : r + 32, :] = green(source[r : r + 32, :])

    def products(k, valid):
        j, i = place(k)
        valid = jnp.where(valid, 1.0, 0.0)
        beside = jnp.where(old + j == i, 0.0, valid).astype(jnp.bfloat16)
        row = block_span(j)
        turned[row, :] += across(table[k], weighted[:, block_span(i)] * valid.astype(jnp.bfloat16))
        field[:, block_span(i)] += down(weighted[:, block_span(old + j)] * beside, table[k])

    field[...] = jnp.zeros_like(field)
    turned[...] = jnp.zeros_like(turned)
    table[0] = jnp.zeros((BLOCK, BLOCK), jnp.bfloat16)
    even[...] = distances(0)

    def pair(t, carry):
        k = 2 * t
        odd[...] = distances(k + 1)
        products(jnp.maximum(k - 1, 0), k > 0)
        fill(k, even)
        even[...] = distances(jnp.minimum(k + 2, count - 1))
        products(k, True)
        fill(k + 1, odd)
        return carry

    lax.fori_loop(0, count // 2, pair, 0)
    if count >= 2:
        products(2 * (count // 2) - 1, True)
    if count % 2:
        fill(count - 1, even)
        products(count - 1, True)
    field[:, old * BLOCK :] += turned[...].T


def prepare(old, data, columns, total, lhs, rhs, weighted, before):
    scaled = lanes(data, 0, 3) * TURNS
    left, right = distance_operands(scaled)
    lhs[...] = left
    rhs[:, old * BLOCK :] = right
    weighted[:, old * BLOCK :] = (lanes(data, 8, columns) * (FOUR_PI / total)).astype(jnp.bfloat16)
    if old:
        rhs[:, : old * BLOCK] = before[0][...]
        weighted[:, : old * BLOCK] = before[1][...]
    return scaled


def strips_kernel(pieces, old, new, columns, total, *refs):
    data, refs = refs[:pieces], refs[pieces:]
    before = refs[: 2 if old else 0]
    table, field, rhs, weighted, lhs, turned, even, odd = refs[len(before) :]
    prepare(old, data, columns, total, lhs, rhs, weighted, before)
    build_strips(old, new, lhs, rhs, weighted, table, field, turned, even, odd)


def iterate_kernel(pieces, new, blocks, columns, groups, *refs):
    data, refs = refs[:pieces], refs[pieces:]
    rest, refs = refs[:new], refs[new:]
    toward_ref, before, refs = refs[0], refs[1:3], refs[3:]
    tables, refs = refs[: len(groups)], refs[len(groups) :]
    fields, refs = refs[: len(groups)], refs[len(groups) :]
    density_out, far_out = refs[:2]
    lhs, rhs, weighted, table, field, turned, even, odd, coords, plane, dens, inc = refs[2:]
    total = blocks * BLOCK
    width = data[0].shape[2]
    old = blocks - new
    prepare(old, rest, columns, total, lhs, rhs, weighted, before)
    build_strips(old, new, lhs, rhs, weighted, table, field, turned, even, odd)

    everything = list(data) + list(rest)
    coords[0:3, :] = lanes(everything, 0, 3) * TURNS
    inverse = 1.0 / lanes(everything, 3, 1)
    dens[...] = lanes(everything, 8, columns)
    inc[...] = lanes(everything, 8 + columns, columns)
    for part in fields:
        field[:, : part.shape[1]] += part[...]
    dens[...] = dens[...] - (field[...] + inc[...]) * inverse

    entries = {}
    for (first, count), part in zip(list(groups) + [(old, new)], list(tables) + [table]):
        k = 0
        for j in range(first, first + count):
            for i in range(j + 1):
                entries[j, i] = (part, k)
                k += 1

    def entry(j, i):
        part, k = entries[j, i]
        return part[k]

    toward = toward_ref[...].T
    cell_area = FOUR_PI / total

    def rounded():
        return (dens[...] * cell_area).astype(jnp.bfloat16)

    def part_of(w, b):
        return w[:, b * BLOCK : (b + 1) * BLOCK]

    steps = ITERS - 1
    per_step = -(-blocks // steps)

    def iterate(step, carry):
        w = rounded()
        for k in range(per_step):
            span = block_span(jnp.minimum(step * per_step + k, blocks - 1))
            phase = toward[:, 0:1] * coords[0:1, span] + toward[:, 1:2] * coords[1:2, span]
            phase = phase + toward[:, 2:3] * coords[2:3, span]
            plane[:, span] = cos_turns(phase, 1.0).astype(jnp.bfloat16)
        downs, sides = [None] * blocks, [None] * blocks
        for b in range(blocks):
            top = blocks - 1 - b
            for n in range(max(blocks - b, top)):
                if b + n < blocks:
                    term = down(part_of(w, b + n), entry(b + n, b))
                    downs[b] = term if n == 0 else downs[b] + term
                if n < top:
                    term = across(entry(top, n), part_of(w, n))
                    sides[top] = term if n == 0 else sides[top] + term
        for b in range(blocks):
            total_field = downs[b] if sides[b] is None else downs[b] + sides[b].T
            span = slice(b * BLOCK, (b + 1) * BLOCK)
            dens[:, span] = dens[:, span] - (total_field + inc[:, span]) * inverse[:, span]
        return carry

    lax.fori_loop(0, steps, iterate, 0)
    density_out[...] = dens[:, 0:width]
    far_out[...] = across(plane[...], rounded()).T


def replicated_shards(points, density, incident, precond, receivers):
    count_tgt = lax.axis_size("tgt")
    count_src = lax.axis_size("src")
    count_sub = lax.axis_size("sub")
    chips = count_tgt * count_src
    columns, width = density.shape
    names = ("tgt", "src", "sub")
    vmem = pl.BlockSpec(memory_space=pltpu.VMEM)
    payload = pl.pallas_call(
        pack_kernel,
        out_shape=jax.ShapeDtypeStruct((8 + 2 * columns, width), jnp.float32),
        in_specs=[pl.BlockSpec(memory_space=pltpu.HBM)] * 4,
        out_specs=vmem,
        scratch_shapes=[pltpu.VMEM((2, 3, width), jnp.float32), pltpu.SemaphoreType.DMA((4,))],
        compiler_params=pltpu.CompilerParams(vmem_limit_bytes=4 * 2**20),
        name="pack",
    )(*(pltpu.with_memory_space_constraint(a, pltpu.HBM) for a in (points, precond[None, :], density, incident)))
    swap = [(0, 1), (1, 0)]
    payload = payload[None]

    def fetch(array, offsets):
        pairs = [(q * 2 + c, (q ^ offsets[c]) * 2 + c) for q in range(chips) for c in range(2)]
        return lax.ppermute(array, names, pairs)

    own = jnp.concatenate([payload, lax.ppermute(payload, "sub", swap)], axis=0)
    near = [fetch(own, (k, k + 1)) for k in range(1, chips - 1, 2)]
    last = fetch(own, (chips - 1, chips - 1))

    place = (lax.axis_index("tgt") * count_src + lax.axis_index("src")) * count_sub + lax.axis_index("sub")
    rows = receivers.shape[0] // (chips * count_sub)
    toward = receiver_directions(lax.dynamic_slice_in_dim(receivers, place * rows, rows, 0))
    toward = jnp.concatenate([toward, jnp.zeros((5, rows), jnp.float32)], axis=0)

    blocks = chips
    total = blocks * BLOCK
    f32, bf16 = jnp.float32, jnp.bfloat16

    def strip_shapes(old, new):
        return [
            ((strip_size(old, new), BLOCK, BLOCK), bf16),
            ((columns, (old + new) * BLOCK), f32),
            ((32, (old + new) * BLOCK), bf16),
            ((columns, (old + new) * BLOCK), bf16),
            ((new * BLOCK, 32), bf16),
            ((new * BLOCK, columns), f32),
            ((BLOCK, BLOCK), f32),
            ((BLOCK, BLOCK), f32),
        ]

    groups, tables, fields, held, before = [], [], [], [], []

    def strips(data):
        old, new = len(held), len(data)
        shapes = strip_shapes(old, new)
        work = strip_size(old, new) * BLOCK * BLOCK
        table, field, *state = pl.pallas_call(
            functools.partial(strips_kernel, new, old, new, columns, total),
            out_shape=[jax.ShapeDtypeStruct(*shape) for shape in shapes[:4]],
            in_specs=[vmem] * (new + len(before)),
            out_specs=[vmem] * 4,
            scratch_shapes=[pltpu.VMEM(*shape) for shape in shapes[4:]],
            compiler_params=pltpu.CompilerParams(vmem_limit_bytes=VMEM_LIMIT),
            cost_estimate=pl.CostEstimate(flops=30 * work, bytes_accessed=2 * work, transcendentals=2 * work),
            name=f"strips{old}",
        )(*data, *before)
        groups.append((old, new))
        tables.append(table)
        fields.append(field)
        held.extend(data)
        before[:] = state

    early, late = near[:2], near[2:]
    swapped = [lax.ppermute(array, "sub", swap) for array in early]
    strips([own] + [array for pair in zip(early, swapped) for array in pair])
    rest = []
    for array in late:
        array, fields[-1] = lax.optimization_barrier((array, fields[-1]))
        other = lax.ppermute(array, "sub", swap)
        strips(rest + [array])
        rest = [other]
    rest.append(last)

    pieces, new = len(held), len(rest)
    shapes = strip_shapes(pieces, new)
    return pl.pallas_call(
        functools.partial(iterate_kernel, pieces, new, blocks, columns, tuple(groups)),
        out_shape=(
            jax.ShapeDtypeStruct((columns, width), f32),
            jax.ShapeDtypeStruct((columns, rows), f32),
        ),
        in_specs=[vmem] * (pieces + new + 3 + 2 * len(groups)),
        out_specs=(vmem, vmem),
        scratch_shapes=[pltpu.VMEM(*shapes[k]) for k in (4, 2, 3, 0, 1, 5, 6, 7)]
        + [
            pltpu.VMEM((8, total), f32),
            pltpu.VMEM((rows, total), bf16),
            pltpu.VMEM((columns, total), f32),
            pltpu.VMEM((columns, total), f32),
        ],
        compiler_params=pltpu.CompilerParams(vmem_limit_bytes=VMEM_LIMIT),
        name="iterate",
    )(*held, *rest, toward, *before, *tables, *fields)


def single_layer(targets, sources):
    delta_x = targets[0][:, None] - sources[0][None, :]
    delta_y = targets[1][:, None] - sources[1][None, :]
    delta_z = targets[2][:, None] - sources[2][None, :]
    squared = delta_x * delta_x + delta_y * delta_y + delta_z * delta_z
    values = jnp.cos(WAVENUMBER * jnp.sqrt(squared)) / (
        FOUR_PI * jnp.sqrt(squared + SMOOTHING * SMOOTHING)
    )
    return values.astype(jnp.bfloat16)


def far_kernel(toward, sources):
    projection = toward[0][:, None] * sources[0][None, :] + toward[1][:, None] * sources[1][None, :]
    projection = projection + toward[2][:, None] * sources[2][None, :]
    return jnp.cos(WAVENUMBER * projection).astype(jnp.bfloat16)


def receiver_directions(direction_index):
    upper_part = direction_index // 256
    lower_part = direction_index % 256
    rotation = (upper_part * 14080 + lower_part * 40503) % 65536
    azimuth = rotation.astype(jnp.float32) * (2.0 * math.pi / 65536.0)
    height = 1.0 - (2 * direction_index + 1).astype(jnp.float32) / NDIR
    radial = jnp.sqrt(jnp.maximum(1.0 - height * height, 0.0))
    return jnp.stack([radial * jnp.cos(azimuth), radial * jnp.sin(azimuth), height])


def fold_blocks(running, incoming, coordinates, targets, maker):
    length = incoming.shape[1]
    block_width = math.gcd(length, 1024)

    def fold_one_block(number, accumulated):
        inside = number * block_width
        part_density = lax.dynamic_slice_in_dim(incoming, inside, block_width, 1)
        part_points = lax.dynamic_slice_in_dim(coordinates, inside, block_width, 1)
        kernel_table = maker(targets, part_points)
        return accumulated + lax.dot_general(
            part_density, kernel_table, (((1,), (1,)), ((), ())), preferred_element_type=jnp.float32
        )

    return lax.fori_loop(0, length // block_width, fold_one_block, running)


def build_table(targets, sources):
    source_count = sources.shape[1]
    block_width = math.gcd(source_count, 1024)
    table = jnp.zeros((targets.shape[1], source_count), jnp.bfloat16)

    def build_one_block(number, filled):
        inside = number * block_width
        part_points = lax.dynamic_slice_in_dim(sources, inside, block_width, 1)
        return lax.dynamic_update_slice_in_dim(
            filled, single_layer(targets, part_points), inside, 1
        )

    return lax.fori_loop(0, source_count // block_width, build_one_block, table)


def shared_shards(points, density, incident, precond, receivers):
    count_tgt = lax.axis_size("tgt")
    count_src = lax.axis_size("src")
    count_sub = lax.axis_size("sub")
    point_count = points.shape[1] * count_tgt * count_src * count_sub
    cell_area = FOUR_PI / point_count
    row_points = lax.all_gather(points, "src", axis=1, tiled=True)
    column_points = lax.all_gather(points, ("tgt", "sub"), axis=1, tiled=True)
    columns_count = density.shape[0]
    stored_table = build_table(row_points, column_points)
    for iteration in range(ITERS):
        weighted = (density * cell_area).astype(jnp.bfloat16)
        partial_sum = lax.dot_general(
            lax.all_gather(weighted, ("tgt", "sub"), axis=1, tiled=True),
            stored_table,
            (((1,), (1,)), ((), ())),
            preferred_element_type=jnp.float32,
        )
        field = lax.psum_scatter(partial_sum, "src", scatter_dimension=1, tiled=True)
        density = density - (field + incident) / precond[None, :]
    weighted = (density * cell_area).astype(jnp.bfloat16)
    receiver_blocks = receivers.reshape(count_tgt, count_src, count_sub, -1)
    picked = lax.dynamic_index_in_dim(receiver_blocks, lax.axis_index("tgt"), 0, keepdims=False)
    picked = lax.dynamic_index_in_dim(picked, lax.axis_index("sub"), 1, keepdims=False)
    toward = receiver_directions(picked.reshape(-1))
    empty_far = jnp.zeros((columns_count, toward.shape[1]), jnp.float32)
    far_partial = fold_blocks(
        empty_far,
        lax.all_gather(weighted, ("tgt", "sub"), axis=1, tiled=True),
        column_points,
        toward,
        far_kernel,
    )
    far_field = lax.psum_scatter(far_partial, "src", scatter_dimension=1, tiled=True)
    return (density, far_field)


def can_replicate(mesh, points):
    sizes = mesh.shape
    chips = sizes["tgt"] * sizes["src"]
    per_group = chips * sizes["sub"]
    total = points.shape[1] // sizes["groups"]
    return (
        sizes["sub"] == 2
        and chips >= 4
        and chips & (chips - 1) == 0
        and total == per_group * (BLOCK // 2)
        and total * total <= TABLE_LIMIT
    )


def solution(mesh):
    placed = (
        P(None, ("groups", "tgt", "src", "sub")),
        P(None, ("groups", "tgt", "src", "sub")),
        P(None, ("groups", "tgt", "src", "sub")),
        P(("groups", "tgt", "src", "sub")),
        P("groups"),
    )

    def whole(points, density, incident, precond, receivers):
        body = replicated_shards if can_replicate(mesh, points) else shared_shards
        return jax.shard_map(
            body,
            mesh=mesh,
            in_specs=placed,
            out_specs=(
                P(None, ("groups", "tgt", "src", "sub")),
                P(None, ("groups", "tgt", "src", "sub")),
            ),
            check_vma=False,
        )(points, density, incident, precond, receivers)

    return whole
```

```python
import functools
import math

import jax
import jax.numpy as jnp
from jax import lax
from jax.experimental import pallas as pl
from jax.experimental.pallas import tpu as pltpu
from jax.sharding import PartitionSpec as P

ITERS = 4
NDIR = 65536


WAVENUMBER = 32.0
SMOOTHING = 0.02
FOUR_PI = 4.0 * math.pi

TURNS = WAVENUMBER / (2.0 * math.pi)
SMOOTH_TURNS = (SMOOTHING * TURNS) ** 2
BLOCK = 256
UNROLL = 4
TABLE_LIMIT = 8 * 2**20
VMEM_LIMIT = 24 * 2**20


def sine_coefficients(count):
    nodes = [0.03125 + 0.03125 * math.cos(math.pi * (k + 0.5) / count) for k in range(count)]
    values = [math.sin(2.0 * math.pi * math.sqrt(u)) / math.sqrt(u) for u in nodes]
    divided = list(values)
    for level in range(1, count):
        for k in range(count - 1, level - 1, -1):
            divided[k] = (divided[k] - divided[k - 1]) / (nodes[k] - nodes[k - level])
    poly = [0.0] * count
    for k in range(count - 1, -1, -1):
        shifted = [0.0] + poly[:-1]
        poly = [s - nodes[k] * p for s, p in zip(shifted, poly)]
        poly[0] += divided[k]
    return poly


SINE = sine_coefficients(4)


def cos_turns(turns, scale):
    folded = 0.25 - jnp.abs(turns - jnp.round(turns))
    square = folded * folded
    value = SINE[-1] * scale
    for c in SINE[-2::-1]:
        value = value * square + c * scale
    return value * folded


def green(squared):
    kept = jnp.maximum(squared, 1e-12)
    turns = kept * lax.rsqrt(kept)
    return (cos_turns(turns, TURNS / FOUR_PI) * lax.rsqrt(squared + SMOOTH_TURNS)).astype(jnp.bfloat16)


def split3(x):
    high = x.astype(jnp.bfloat16).astype(jnp.float32)
    rest = x - high
    mid = rest.astype(jnp.bfloat16).astype(jnp.float32)
    low = (rest - mid).astype(jnp.bfloat16).astype(jnp.float32)
    return high, mid, low


def pack_kernel(points, precond, density, incident, out, head, sems):
    columns = density.shape[0]
    moves = [
        (points, head.at[0]),
        (precond, head.at[1, pl.ds(0, 1)]),
        (density, out.at[pl.ds(8, columns)]),
        (incident, out.at[pl.ds(8 + columns, columns)]),
    ]
    copies = [pltpu.make_async_copy(src, dst, sems.at[k]) for k, (src, dst) in enumerate(moves)]
    for copy in copies:
        copy.start()
    copies[0].wait()
    copies[1].wait()
    out[0:3, :] = head[0]
    out[3:4, :] = head[1, 0:1]
    out[4:8, :] = jnp.zeros((4, out.shape[1]), jnp.float32)
    copies[2].wait()
    copies[3].wait()


def lanes(data, start, count):
    return jnp.concatenate(
        [piece[s, start : start + count, :] for piece in data for s in range(piece.shape[0])], axis=1
    )


def distance_operands(scaled):
    ones = jnp.ones((1, scaled.shape[1]), jnp.float32)
    left, right = [], []
    for k in range(3):
        h, m, l = split3(scaled[k : k + 1])
        left += [-2.0 * h, -2.0 * h, -2.0 * m, -2.0 * m, -2.0 * h, -2.0 * l]
        right += [h, m, h, m, l, h]
    norm = scaled[0:1] * scaled[0:1] + scaled[1:2] * scaled[1:2] + scaled[2:3] * scaled[2:3]
    h, m, l = split3(norm)
    left += [h, m, l, ones, ones, ones]
    right += [ones, ones, ones, h, m, l]
    zeros = jnp.zeros((8, scaled.shape[1]), jnp.float32)
    left = jnp.concatenate(left + [zeros], axis=0)
    right = jnp.concatenate(right + [zeros], axis=0).astype(jnp.bfloat16)
    return left.T.astype(jnp.bfloat16), right


def down(w, kernel_block):
    return lax.dot_general(w, kernel_block, (((1,), (0,)), ((), ())), preferred_element_type=jnp.float32)


def across(kernel_block, w):
    return lax.dot_general(kernel_block, w, (((1,), (1,)), ((), ())), preferred_element_type=jnp.float32)


def block_span(index):
    return pl.ds(pl.multiple_of(index * BLOCK, BLOCK), BLOCK)


def strip_size(old, new):
    return sum(j + 1 for j in range(old, old + new))


def build_strips(old, new, lhs, rhs, weighted, table, field, turned, even, odd):
    count = strip_size(old, new)
    starts = [strip_size(old, k) for k in range(new)]

    def place(k):
        j, i = 0, k
        for step in range(1, new):
            past = k >= starts[step]
            j = jnp.where(past, step, j)
            i = jnp.where(past, k - starts[step], i)
        return j, i

    def distances(k):
        j, i = place(k)
        return lax.dot_general(
            lhs[block_span(j), :], rhs[:, block_span(i)], (((1,), (0,)), ((), ())), preferred_element_type=jnp.float32
        )

    def fill(k, source):
        for r in range(0, BLOCK, 32):
            table[k, r : r + 32, :] = green(source[r : r + 32, :])

    def products(k, valid):
        j, i = place(k)
        valid = jnp.where(valid, 1.0, 0.0)
        beside = jnp.where(old + j == i, 0.0, valid).astype(jnp.bfloat16)
        row = block_span(j)
        turned[row, :] += across(table[k], weighted[:, block_span(i)] * valid.astype(jnp.bfloat16))
        field[:, block_span(i)] += down(weighted[:, block_span(old + j)] * beside, table[k])

    field[...] = jnp.zeros_like(field)
    turned[...] = jnp.zeros_like(turned)
    table[0] = jnp.zeros((BLOCK, BLOCK), jnp.bfloat16)
    stage = (even, odd)
    even[...] = distances(0)

    def several(t, carry):
        k = UNROLL * t
        for n in range(UNROLL):
            stage[(n + 1) % 2][...] = distances(jnp.minimum(k + n + 1, count - 1))
            if n == 0:
                products(jnp.maximum(k - 1, 0), k > 0)
            else:
                products(k + n - 1, True)
            fill(k + n, stage[n % 2])
        return carry

    lax.fori_loop(0, count // UNROLL, several, 0)
    for n, k in enumerate(range(count // UNROLL * UNROLL, count)):
        if k + 1 < count:
            stage[(n + 1) % 2][...] = distances(k + 1)
        if k:
            products(k - 1, True)
        fill(k, stage[n % 2])
    products(count - 1, True)
    field[:, old * BLOCK :] += turned[...].T


def prepare(old, data, columns, total, lhs, rhs, weighted, before):
    scaled = lanes(data, 0, 3) * TURNS
    left, right = distance_operands(scaled)
    lhs[...] = left
    rhs[:, old * BLOCK :] = right
    weighted[:, old * BLOCK :] = (lanes(data, 8, columns) * (FOUR_PI / total)).astype(jnp.bfloat16)
    if old:
        rhs[:, : old * BLOCK] = before[0][...]
        weighted[:, : old * BLOCK] = before[1][...]
    return scaled


def strips_kernel(pieces, old, new, columns, total, *refs):
    data, refs = refs[:pieces], refs[pieces:]
    before = refs[: 2 if old else 0]
    table, field, rhs, weighted, lhs, turned, even, odd = refs[len(before) :]
    prepare(old, data, columns, total, lhs, rhs, weighted, before)
    build_strips(old, new, lhs, rhs, weighted, table, field, turned, even, odd)


def iterate_kernel(pieces, new, blocks, columns, groups, *refs):
    data, refs = refs[:pieces], refs[pieces:]
    rest, refs = refs[:new], refs[new:]
    toward_ref, before, refs = refs[0], refs[1:3], refs[3:]
    tables, refs = refs[: len(groups)], refs[len(groups) :]
    fields, refs = refs[: len(groups)], refs[len(groups) :]
    density_out, far_out = refs[:2]
    lhs, rhs, weighted, table, field, turned, even, odd, coords, plane, dens, inc = refs[2:]
    total = blocks * BLOCK
    width = data[0].shape[2]
    old = blocks - new
    prepare(old, rest, columns, total, lhs, rhs, weighted, before)
    build_strips(old, new, lhs, rhs, weighted, table, field, turned, even, odd)

    everything = list(data) + list(rest)
    coords[0:3, :] = lanes(everything, 0, 3) * TURNS
    inverse = 1.0 / lanes(everything, 3, 1)
    dens[...] = lanes(everything, 8, columns)
    inc[...] = lanes(everything, 8 + columns, columns)
    for part in fields:
        field[:, : part.shape[1]] += part[...]
    dens[...] = dens[...] - (field[...] + inc[...]) * inverse

    entries = {}
    for (first, count), part in zip(list(groups) + [(old, new)], list(tables) + [table]):
        k = 0
        for j in range(first, first + count):
            for i in range(j + 1):
                entries[j, i] = (part, k)
                k += 1

    def entry(j, i):
        part, k = entries[j, i]
        return part[k]

    toward = toward_ref[...].T
    cell_area = FOUR_PI / total

    def rounded():
        return (dens[...] * cell_area).astype(jnp.bfloat16)

    def part_of(w, b):
        return w[:, b * BLOCK : (b + 1) * BLOCK]

    steps = ITERS - 1
    per_step = -(-blocks // steps)

    def iterate(step, carry):
        w = rounded()
        for k in range(per_step):
            span = block_span(jnp.minimum(step * per_step + k, blocks - 1))
            phase = toward[:, 0:1] * coords[0:1, span] + toward[:, 1:2] * coords[1:2, span]
            phase = phase + toward[:, 2:3] * coords[2:3, span]
            plane[:, span] = cos_turns(phase, 1.0).astype(jnp.bfloat16)
        downs, sides = [None] * blocks, [None] * blocks
        for b in range(blocks):
            top = blocks - 1 - b
            for n in range(max(blocks - b, top)):
                if b + n < blocks:
                    term = down(part_of(w, b + n), entry(b + n, b))
                    downs[b] = term if n == 0 else downs[b] + term
                if n < top:
                    term = across(entry(top, n), part_of(w, n))
                    sides[top] = term if n == 0 else sides[top] + term
        for b in range(blocks):
            total_field = downs[b] if sides[b] is None else downs[b] + sides[b].T
            span = slice(b * BLOCK, (b + 1) * BLOCK)
            dens[:, span] = dens[:, span] - (total_field + inc[:, span]) * inverse[:, span]
        return carry

    lax.fori_loop(0, steps, iterate, 0)
    density_out[...] = dens[:, 0:width]
    far_out[...] = across(plane[...], rounded()).T


def replicated_shards(points, density, incident, precond, receivers):
    count_tgt = lax.axis_size("tgt")
    count_src = lax.axis_size("src")
    count_sub = lax.axis_size("sub")
    chips = count_tgt * count_src
    columns, width = density.shape
    names = ("tgt", "src", "sub")
    vmem = pl.BlockSpec(memory_space=pltpu.VMEM)
    payload = pl.pallas_call(
        pack_kernel,
        out_shape=jax.ShapeDtypeStruct((8 + 2 * columns, width), jnp.float32),
        in_specs=[pl.BlockSpec(memory_space=pltpu.HBM)] * 4,
        out_specs=vmem,
        scratch_shapes=[pltpu.VMEM((2, 3, width), jnp.float32), pltpu.SemaphoreType.DMA((4,))],
        compiler_params=pltpu.CompilerParams(vmem_limit_bytes=4 * 2**20),
        name="pack",
    )(*(pltpu.with_memory_space_constraint(a, pltpu.HBM) for a in (points, precond[None, :], density, incident)))
    swap = [(0, 1), (1, 0)]
    payload = payload[None]

    def fetch(array, offsets):
        pairs = [(q * 2 + c, (q ^ offsets[c]) * 2 + c) for q in range(chips) for c in range(2)]
        return lax.ppermute(array, names, pairs)

    far = fetch(payload, (chips - 1, chips - 1))
    own = jnp.concatenate([payload, lax.ppermute(payload, "sub", swap)], axis=0)
    near = [fetch(own, (k, k + 1)) for k in range(1, chips - 1, 2)]

    place = (lax.axis_index("tgt") * count_src + lax.axis_index("src")) * count_sub + lax.axis_index("sub")
    rows = receivers.shape[0] // (chips * count_sub)
    toward = receiver_directions(lax.dynamic_slice_in_dim(receivers, place * rows, rows, 0))
    toward = jnp.concatenate([toward, jnp.zeros((5, rows), jnp.float32)], axis=0)

    blocks = chips
    total = blocks * BLOCK
    f32, bf16 = jnp.float32, jnp.bfloat16

    def strip_shapes(old, new):
        return [
            ((strip_size(old, new), BLOCK, BLOCK), bf16),
            ((columns, (old + new) * BLOCK), f32),
            ((32, (old + new) * BLOCK), bf16),
            ((columns, (old + new) * BLOCK), bf16),
            ((new * BLOCK, 32), bf16),
            ((new * BLOCK, columns), f32),
            ((BLOCK, BLOCK), f32),
            ((BLOCK, BLOCK), f32),
        ]

    groups, tables, fields, held, before = [], [], [], [], []

    def strips(data):
        old, new = (sum(array.shape[0] for array in arrays) // 2 for arrays in (held, data))
        shapes = strip_shapes(old, new)
        work = strip_size(old, new) * BLOCK * BLOCK
        table, field, *state = pl.pallas_call(
            functools.partial(strips_kernel, len(data), old, new, columns, total),
            out_shape=[jax.ShapeDtypeStruct(*shape) for shape in shapes[:4]],
            in_specs=[vmem] * (len(data) + len(before)),
            out_specs=[vmem] * 4,
            scratch_shapes=[pltpu.VMEM(*shape) for shape in shapes[4:]],
            compiler_params=pltpu.CompilerParams(vmem_limit_bytes=VMEM_LIMIT),
            cost_estimate=pl.CostEstimate(flops=30 * work, bytes_accessed=2 * work, transcendentals=2 * work),
            name=f"strips{old}",
        )(*data, *before)
        groups.append((old, new))
        tables.append(table)
        fields.append(field)
        held.extend(data)
        before[:] = state

    def both(array):
        return [array, lax.ppermute(array, "sub", swap)]

    def swapped(array):
        return lax.ppermute(array, "sub", swap)

    first, late = [own, far, swapped(far)], near
    if len(near) > 1:
        first[1:1] = [near[0], swapped(near[0])]
        late = near[1:]
    strips(first)
    *late, fields[0] = lax.optimization_barrier((*late, fields[0]))
    rest = [swapped(array) for array in late]
    strips(late)
    pieces, new = len(held), len(rest)
    shapes = strip_shapes(blocks - new, new)
    return pl.pallas_call(
        functools.partial(iterate_kernel, pieces, new, blocks, columns, tuple(groups)),
        out_shape=(
            jax.ShapeDtypeStruct((columns, width), f32),
            jax.ShapeDtypeStruct((columns, rows), f32),
        ),
        in_specs=[vmem] * (pieces + new + 3 + 2 * len(groups)),
        out_specs=(vmem, vmem),
        scratch_shapes=[pltpu.VMEM(*shapes[k]) for k in (4, 2, 3, 0, 1, 5, 6, 7)]
        + [
            pltpu.VMEM((8, total), f32),
            pltpu.VMEM((rows, total), bf16),
            pltpu.VMEM((columns, total), f32),
            pltpu.VMEM((columns, total), f32),
        ],
        compiler_params=pltpu.CompilerParams(vmem_limit_bytes=VMEM_LIMIT),
        name="iterate",
    )(*held, *rest, toward, *before, *tables, *fields)


def single_layer(targets, sources):
    delta_x = targets[0][:, None] - sources[0][None, :]
    delta_y = targets[1][:, None] - sources[1][None, :]
    delta_z = targets[2][:, None] - sources[2][None, :]
    squared = delta_x * delta_x + delta_y * delta_y + delta_z * delta_z
    values = jnp.cos(WAVENUMBER * jnp.sqrt(squared)) / (
        FOUR_PI * jnp.sqrt(squared + SMOOTHING * SMOOTHING)
    )
    return values.astype(jnp.bfloat16)


def far_kernel(toward, sources):
    projection = toward[0][:, None] * sources[0][None, :] + toward[1][:, None] * sources[1][None, :]
    projection = projection + toward[2][:, None] * sources[2][None, :]
    return jnp.cos(WAVENUMBER * projection).astype(jnp.bfloat16)


def receiver_directions(direction_index):
    upper_part = direction_index // 256
    lower_part = direction_index % 256
    rotation = (upper_part * 14080 + lower_part * 40503) % 65536
    azimuth = rotation.astype(jnp.float32) * (2.0 * math.pi / 65536.0)
    height = 1.0 - (2 * direction_index + 1).astype(jnp.float32) / NDIR
    radial = jnp.sqrt(jnp.maximum(1.0 - height * height, 0.0))
    return jnp.stack([radial * jnp.cos(azimuth), radial * jnp.sin(azimuth), height])


def fold_blocks(running, incoming, coordinates, targets, maker):
    length = incoming.shape[1]
    block_width = math.gcd(length, 1024)

    def fold_one_block(number, accumulated):
        inside = number * block_width
        part_density = lax.dynamic_slice_in_dim(incoming, inside, block_width, 1)
        part_points = lax.dynamic_slice_in_dim(coordinates, inside, block_width, 1)
        kernel_table = maker(targets, part_points)
        return accumulated + lax.dot_general(
            part_density, kernel_table, (((1,), (1,)), ((), ())), preferred_element_type=jnp.float32
        )

    return lax.fori_loop(0, length // block_width, fold_one_block, running)


def build_table(targets, sources):
    source_count = sources.shape[1]
    block_width = math.gcd(source_count, 1024)
    table = jnp.zeros((targets.shape[1], source_count), jnp.bfloat16)

    def build_one_block(number, filled):
        inside = number * block_width
        part_points = lax.dynamic_slice_in_dim(sources, inside, block_width, 1)
        return lax.dynamic_update_slice_in_dim(
            filled, single_layer(targets, part_points), inside, 1
        )

    return lax.fori_loop(0, source_count // block_width, build_one_block, table)


def shared_shards(points, density, incident, precond, receivers):
    count_tgt = lax.axis_size("tgt")
    count_src = lax.axis_size("src")
    count_sub = lax.axis_size("sub")
    point_count = points.shape[1] * count_tgt * count_src * count_sub
    cell_area = FOUR_PI / point_count
    row_points = lax.all_gather(points, "src", axis=1, tiled=True)
    column_points = lax.all_gather(points, ("tgt", "sub"), axis=1, tiled=True)
    columns_count = density.shape[0]
    stored_table = build_table(row_points, column_points)
    for iteration in range(ITERS):
        weighted = (density * cell_area).astype(jnp.bfloat16)
        partial_sum = lax.dot_general(
            lax.all_gather(weighted, ("tgt", "sub"), axis=1, tiled=True),
            stored_table,
            (((1,), (1,)), ((), ())),
            preferred_element_type=jnp.float32,
        )
        field = lax.psum_scatter(partial_sum, "src", scatter_dimension=1, tiled=True)
        density = density - (field + incident) / precond[None, :]
    weighted = (density * cell_area).astype(jnp.bfloat16)
    receiver_blocks = receivers.reshape(count_tgt, count_src, count_sub, -1)
    picked = lax.dynamic_index_in_dim(receiver_blocks, lax.axis_index("tgt"), 0, keepdims=False)
    picked = lax.dynamic_index_in_dim(picked, lax.axis_index("sub"), 1, keepdims=False)
    toward = receiver_directions(picked.reshape(-1))
    empty_far = jnp.zeros((columns_count, toward.shape[1]), jnp.float32)
    far_partial = fold_blocks(
        empty_far,
        lax.all_gather(weighted, ("tgt", "sub"), axis=1, tiled=True),
        column_points,
        toward,
        far_kernel,
    )
    far_field = lax.psum_scatter(far_partial, "src", scatter_dimension=1, tiled=True)
    return (density, far_field)


def can_replicate(mesh, points):
    sizes = mesh.shape
    chips = sizes["tgt"] * sizes["src"]
    per_group = chips * sizes["sub"]
    total = points.shape[1] // sizes["groups"]
    return (
        sizes["sub"] == 2
        and chips >= 4
        and chips & (chips - 1) == 0
        and total == per_group * (BLOCK // 2)
        and total * total <= TABLE_LIMIT
    )


def solution(mesh):
    placed = (
        P(None, ("groups", "tgt", "src", "sub")),
        P(None, ("groups", "tgt", "src", "sub")),
        P(None, ("groups", "tgt", "src", "sub")),
        P(("groups", "tgt", "src", "sub")),
        P("groups"),
    )

    def whole(points, density, incident, precond, receivers):
        body = replicated_shards if can_replicate(mesh, points) else shared_shards
        return jax.shard_map(
            body,
            mesh=mesh,
            in_specs=placed,
            out_specs=(
                P(None, ("groups", "tgt", "src", "sub")),
                P(None, ("groups", "tgt", "src", "sub")),
            ),
            check_vma=False,
        )(points, density, incident, precond, receivers)

    return whole
```

```python
import functools
import math

import jax
import jax.numpy as jnp
from jax import lax
from jax.experimental import pallas as pl
from jax.experimental.pallas import tpu as pltpu
from jax.sharding import PartitionSpec as P

ITERS = 4
NDIR = 65536


WAVENUMBER = 32.0
SMOOTHING = 0.02
FOUR_PI = 4.0 * math.pi

TURNS = WAVENUMBER / (2.0 * math.pi)
SMOOTH_TURNS = (SMOOTHING * TURNS) ** 2
BLOCK = 256
UNROLL = 4
TABLE_LIMIT = 8 * 2**20
VMEM_LIMIT = 24 * 2**20


def sine_coefficients(count):
    nodes = [0.03125 + 0.03125 * math.cos(math.pi * (k + 0.5) / count) for k in range(count)]
    values = [math.sin(2.0 * math.pi * math.sqrt(u)) / math.sqrt(u) for u in nodes]
    divided = list(values)
    for level in range(1, count):
        for k in range(count - 1, level - 1, -1):
            divided[k] = (divided[k] - divided[k - 1]) / (nodes[k] - nodes[k - level])
    poly = [0.0] * count
    for k in range(count - 1, -1, -1):
        shifted = [0.0] + poly[:-1]
        poly = [s - nodes[k] * p for s, p in zip(shifted, poly)]
        poly[0] += divided[k]
    return poly


SINE = sine_coefficients(4)


def cos_turns(turns, scale):
    folded = 0.25 - jnp.abs(turns - jnp.round(turns))
    square = folded * folded
    value = SINE[-1] * scale
    for c in SINE[-2::-1]:
        value = value * square + c * scale
    return value * folded


def green(squared):
    kept = jnp.maximum(squared, 1e-12)
    turns = kept * lax.rsqrt(kept)
    return (cos_turns(turns, TURNS / FOUR_PI) * lax.rsqrt(squared + SMOOTH_TURNS)).astype(jnp.bfloat16)


def split3(x):
    high = x.astype(jnp.bfloat16).astype(jnp.float32)
    rest = x - high
    mid = rest.astype(jnp.bfloat16).astype(jnp.float32)
    low = (rest - mid).astype(jnp.bfloat16).astype(jnp.float32)
    return high, mid, low


def pack_kernel(points, precond, density, incident, receivers, out, picked, head, sems):
    columns = density.shape[0]
    chip = lax.axis_index("tgt") * lax.axis_size("src") + lax.axis_index("src")
    place = chip * lax.axis_size("sub") + lax.axis_index("sub")
    moves = [
        (points, head.at[0]),
        (precond, head.at[1, pl.ds(0, 1)]),
        (density, out.at[pl.ds(8, columns)]),
        (incident, out.at[pl.ds(8 + columns, columns)]),
        (receivers.at[pl.ds(place, 1)], picked),
    ]
    copies = [pltpu.make_async_copy(src, dst, sems.at[k]) for k, (src, dst) in enumerate(moves)]
    for copy in copies:
        copy.start()
    copies[0].wait()
    copies[1].wait()
    out[0:3, :] = head[0]
    out[3:4, :] = head[1, 0:1]
    out[4:8, :] = jnp.zeros((4, out.shape[1]), jnp.float32)
    for copy in copies[2:]:
        copy.wait()


def lanes(data, start, count):
    return jnp.concatenate(
        [piece[s, start : start + count, :] for piece in data for s in range(piece.shape[0])], axis=1
    )


def distance_operands(scaled):
    ones = jnp.ones((1, scaled.shape[1]), jnp.float32)
    left, right = [], []
    for k in range(3):
        h, m, l = split3(scaled[k : k + 1])
        left += [-2.0 * h, -2.0 * h, -2.0 * m, -2.0 * m, -2.0 * h, -2.0 * l]
        right += [h, m, h, m, l, h]
    norm = scaled[0:1] * scaled[0:1] + scaled[1:2] * scaled[1:2] + scaled[2:3] * scaled[2:3]
    h, m, l = split3(norm)
    left += [h, m, l, ones, ones, ones]
    right += [ones, ones, ones, h, m, l]
    zeros = jnp.zeros((8, scaled.shape[1]), jnp.float32)
    left = jnp.concatenate(left + [zeros], axis=0)
    right = jnp.concatenate(right + [zeros], axis=0).astype(jnp.bfloat16)
    return left.T.astype(jnp.bfloat16), right


def down(w, kernel_block):
    return lax.dot_general(w, kernel_block, (((1,), (0,)), ((), ())), preferred_element_type=jnp.float32)


def across(kernel_block, w):
    return lax.dot_general(kernel_block, w, (((1,), (1,)), ((), ())), preferred_element_type=jnp.float32)


def block_span(index):
    return pl.ds(pl.multiple_of(index * BLOCK, BLOCK), BLOCK)


def strip_size(old, new):
    return sum(j + 1 for j in range(old, old + new))


def build_strips(old, new, lhs, rhs, weighted, table, field, turned, even, odd):
    count = strip_size(old, new)
    starts = [strip_size(old, k) for k in range(new)]

    def place(k):
        j, i = 0, k
        for step in range(1, new):
            past = k >= starts[step]
            j = jnp.where(past, step, j)
            i = jnp.where(past, k - starts[step], i)
        return j, i

    def distances(k):
        j, i = place(k)
        return lax.dot_general(
            lhs[block_span(j), :], rhs[:, block_span(i)], (((1,), (0,)), ((), ())), preferred_element_type=jnp.float32
        )

    def fill(k, source):
        for r in range(0, BLOCK, 32):
            table[k, r : r + 32, :] = green(source[r : r + 32, :])

    def products(k, valid):
        j, i = place(k)
        valid = jnp.where(valid, 1.0, 0.0)
        beside = jnp.where(old + j == i, 0.0, valid).astype(jnp.bfloat16)
        row = block_span(j)
        turned[row, :] += across(table[k], weighted[:, block_span(i)] * valid.astype(jnp.bfloat16))
        field[:, block_span(i)] += down(weighted[:, block_span(old + j)] * beside, table[k])

    field[...] = jnp.zeros_like(field)
    turned[...] = jnp.zeros_like(turned)
    table[0] = jnp.zeros((BLOCK, BLOCK), jnp.bfloat16)
    stage = (even, odd)
    even[...] = distances(0)

    def several(t, carry):
        k = UNROLL * t
        for n in range(UNROLL):
            stage[(n + 1) % 2][...] = distances(jnp.minimum(k + n + 1, count - 1))
            if n == 0:
                products(jnp.maximum(k - 1, 0), k > 0)
            else:
                products(k + n - 1, True)
            fill(k + n, stage[n % 2])
        return carry

    lax.fori_loop(0, count // UNROLL, several, 0)
    for n, k in enumerate(range(count // UNROLL * UNROLL, count)):
        if k + 1 < count:
            stage[(n + 1) % 2][...] = distances(k + 1)
        if k:
            products(k - 1, True)
        fill(k, stage[n % 2])
    products(count - 1, True)
    field[:, old * BLOCK :] += turned[...].T


def prepare(old, data, columns, total, lhs, rhs, weighted, before):
    scaled = lanes(data, 0, 3) * TURNS
    left, right = distance_operands(scaled)
    lhs[...] = left
    rhs[:, old * BLOCK :] = right
    weighted[:, old * BLOCK :] = (lanes(data, 8, columns) * (FOUR_PI / total)).astype(jnp.bfloat16)
    if old:
        rhs[:, : old * BLOCK] = before[0][...]
        weighted[:, : old * BLOCK] = before[1][...]
    return scaled


def strips_kernel(pieces, old, new, columns, total, *refs):
    data, refs = refs[:pieces], refs[pieces:]
    before = refs[: 2 if old else 0]
    table, field, rhs, weighted, lhs, turned, even, odd = refs[len(before) :]
    prepare(old, data, columns, total, lhs, rhs, weighted, before)
    build_strips(old, new, lhs, rhs, weighted, table, field, turned, even, odd)


def iterate_kernel(pieces, new, blocks, columns, groups, *refs):
    data, refs = refs[:pieces], refs[pieces:]
    rest, refs = refs[:new], refs[new:]
    toward_ref, before, refs = refs[0], refs[1:3], refs[3:]
    tables, refs = refs[: len(groups)], refs[len(groups) :]
    fields, refs = refs[: len(groups)], refs[len(groups) :]
    density_out, far_out = refs[:2]
    lhs, rhs, weighted, table, field, turned, even, odd, coords, plane, dens, inc = refs[2:]
    total = blocks * BLOCK
    width = data[0].shape[2]
    old = blocks - new
    prepare(old, rest, columns, total, lhs, rhs, weighted, before)
    build_strips(old, new, lhs, rhs, weighted, table, field, turned, even, odd)

    everything = list(data) + list(rest)
    coords[0:3, :] = lanes(everything, 0, 3) * TURNS
    inverse = 1.0 / lanes(everything, 3, 1)
    dens[...] = lanes(everything, 8, columns)
    inc[...] = lanes(everything, 8 + columns, columns)
    for part in fields:
        field[:, : part.shape[1]] += part[...]
    dens[...] = dens[...] - (field[...] + inc[...]) * inverse

    entries = {}
    for (first, count), part in zip(list(groups) + [(old, new)], list(tables) + [table]):
        k = 0
        for j in range(first, first + count):
            for i in range(j + 1):
                entries[j, i] = (part, k)
                k += 1

    def entry(j, i):
        part, k = entries[j, i]
        return part[k]

    toward = toward_ref[...].T
    cell_area = FOUR_PI / total

    def rounded():
        return (dens[...] * cell_area).astype(jnp.bfloat16)

    def part_of(w, b):
        return w[:, b * BLOCK : (b + 1) * BLOCK]

    steps = ITERS - 1
    per_step = -(-blocks // steps)

    def iterate(step, carry):
        w = rounded()
        for k in range(per_step):
            span = block_span(jnp.minimum(step * per_step + k, blocks - 1))
            phase = toward[:, 0:1] * coords[0:1, span] + toward[:, 1:2] * coords[1:2, span]
            phase = phase + toward[:, 2:3] * coords[2:3, span]
            plane[:, span] = cos_turns(phase, 1.0).astype(jnp.bfloat16)
        downs, sides = [None] * blocks, [None] * blocks
        for b in range(blocks):
            top = blocks - 1 - b
            for n in range(max(blocks - b, top)):
                if b + n < blocks:
                    term = down(part_of(w, b + n), entry(b + n, b))
                    downs[b] = term if n == 0 else downs[b] + term
                if n < top:
                    term = across(entry(top, n), part_of(w, n))
                    sides[top] = term if n == 0 else sides[top] + term
        for b in range(blocks):
            total_field = downs[b] if sides[b] is None else downs[b] + sides[b].T
            span = slice(b * BLOCK, (b + 1) * BLOCK)
            dens[:, span] = dens[:, span] - (total_field + inc[:, span]) * inverse[:, span]
        return carry

    lax.fori_loop(0, steps, iterate, 0)
    density_out[...] = dens[:, 0:width]
    far_out[...] = across(plane[...], rounded()).T


def replicated_shards(points, density, incident, precond, receivers):
    count_tgt = lax.axis_size("tgt")
    count_src = lax.axis_size("src")
    count_sub = lax.axis_size("sub")
    chips = count_tgt * count_src
    columns, width = density.shape
    names = ("tgt", "src", "sub")
    vmem = pl.BlockSpec(memory_space=pltpu.VMEM)
    rows = receivers.shape[0] // (chips * count_sub)
    inputs = (points, precond[None, :], density, incident, receivers.reshape(-1, rows))
    payload, picked = pl.pallas_call(
        pack_kernel,
        out_shape=(
            jax.ShapeDtypeStruct((8 + 2 * columns, width), jnp.float32),
            jax.ShapeDtypeStruct((1, rows), jnp.int32),
        ),
        in_specs=[pl.BlockSpec(memory_space=pltpu.HBM)] * len(inputs),
        out_specs=(vmem, vmem),
        scratch_shapes=[pltpu.VMEM((2, 3, width), jnp.float32), pltpu.SemaphoreType.DMA((len(inputs),))],
        compiler_params=pltpu.CompilerParams(vmem_limit_bytes=4 * 2**20),
        name="pack",
    )(*(pltpu.with_memory_space_constraint(array, pltpu.HBM) for array in inputs))
    swap = [(0, 1), (1, 0)]
    payload = payload[None]

    def fetch(array, offsets):
        pairs = [(q * 2 + c, (q ^ offsets[c]) * 2 + c) for q in range(chips) for c in range(2)]
        return lax.ppermute(array, names, pairs)

    far = fetch(payload, (chips - 1, chips - 1))
    own = jnp.concatenate([payload, lax.ppermute(payload, "sub", swap)], axis=0)
    near = [fetch(own, (k, k + 1)) for k in range(1, chips - 1, 2)]

    toward = receiver_directions(picked[0])
    toward = jnp.concatenate([toward, jnp.zeros((5, rows), jnp.float32)], axis=0)

    blocks = chips
    total = blocks * BLOCK
    f32, bf16 = jnp.float32, jnp.bfloat16

    def strip_shapes(old, new):
        return [
            ((strip_size(old, new), BLOCK, BLOCK), bf16),
            ((columns, (old + new) * BLOCK), f32),
            ((32, (old + new) * BLOCK), bf16),
            ((columns, (old + new) * BLOCK), bf16),
            ((new * BLOCK, 32), bf16),
            ((new * BLOCK, columns), f32),
            ((BLOCK, BLOCK), f32),
            ((BLOCK, BLOCK), f32),
        ]

    groups, tables, fields, held, before = [], [], [], [], []

    def strips(data):
        old, new = (sum(array.shape[0] for array in arrays) // 2 for arrays in (held, data))
        shapes = strip_shapes(old, new)
        work = strip_size(old, new) * BLOCK * BLOCK
        table, field, *state = pl.pallas_call(
            functools.partial(strips_kernel, len(data), old, new, columns, total),
            out_shape=[jax.ShapeDtypeStruct(*shape) for shape in shapes[:4]],
            in_specs=[vmem] * (len(data) + len(before)),
            out_specs=[vmem] * 4,
            scratch_shapes=[pltpu.VMEM(*shape) for shape in shapes[4:]],
            compiler_params=pltpu.CompilerParams(vmem_limit_bytes=VMEM_LIMIT),
            cost_estimate=pl.CostEstimate(flops=30 * work, bytes_accessed=2 * work, transcendentals=2 * work),
            name=f"strips{old}",
        )(*data, *before)
        groups.append((old, new))
        tables.append(table)
        fields.append(field)
        held.extend(data)
        before[:] = state

    def both(array):
        return [array, lax.ppermute(array, "sub", swap)]

    def swapped(array):
        return lax.ppermute(array, "sub", swap)

    first, late = [own, far, swapped(far)], near
    if len(near) > 1:
        first[1:1] = [near[0], swapped(near[0])]
        late = near[1:]
    strips(first)
    *late, fields[0] = lax.optimization_barrier((*late, fields[0]))
    rest = [swapped(array) for array in late]
    strips(late)
    pieces, new = len(held), len(rest)
    shapes = strip_shapes(blocks - new, new)
    return pl.pallas_call(
        functools.partial(iterate_kernel, pieces, new, blocks, columns, tuple(groups)),
        out_shape=(
            jax.ShapeDtypeStruct((columns, width), f32),
            jax.ShapeDtypeStruct((columns, rows), f32),
        ),
        in_specs=[vmem] * (pieces + new + 3 + 2 * len(groups)),
        out_specs=(vmem, vmem),
        scratch_shapes=[pltpu.VMEM(*shapes[k]) for k in (4, 2, 3, 0, 1, 5, 6, 7)]
        + [
            pltpu.VMEM((8, total), f32),
            pltpu.VMEM((rows, total), bf16),
            pltpu.VMEM((columns, total), f32),
            pltpu.VMEM((columns, total), f32),
        ],
        compiler_params=pltpu.CompilerParams(vmem_limit_bytes=VMEM_LIMIT),
        name="iterate",
    )(*held, *rest, toward, *before, *tables, *fields)


def single_layer(targets, sources):
    delta_x = targets[0][:, None] - sources[0][None, :]
    delta_y = targets[1][:, None] - sources[1][None, :]
    delta_z = targets[2][:, None] - sources[2][None, :]
    squared = delta_x * delta_x + delta_y * delta_y + delta_z * delta_z
    values = jnp.cos(WAVENUMBER * jnp.sqrt(squared)) / (
        FOUR_PI * jnp.sqrt(squared + SMOOTHING * SMOOTHING)
    )
    return values.astype(jnp.bfloat16)


def far_kernel(toward, sources):
    projection = toward[0][:, None] * sources[0][None, :] + toward[1][:, None] * sources[1][None, :]
    projection = projection + toward[2][:, None] * sources[2][None, :]
    return jnp.cos(WAVENUMBER * projection).astype(jnp.bfloat16)


def receiver_directions(direction_index):
    upper_part = direction_index // 256
    lower_part = direction_index % 256
    rotation = (upper_part * 14080 + lower_part * 40503) % 65536
    azimuth = rotation.astype(jnp.float32) * (2.0 * math.pi / 65536.0)
    height = 1.0 - (2 * direction_index + 1).astype(jnp.float32) / NDIR
    radial = jnp.sqrt(jnp.maximum(1.0 - height * height, 0.0))
    return jnp.stack([radial * jnp.cos(azimuth), radial * jnp.sin(azimuth), height])


def fold_blocks(running, incoming, coordinates, targets, maker):
    length = incoming.shape[1]
    block_width = math.gcd(length, 1024)

    def fold_one_block(number, accumulated):
        inside = number * block_width
        part_density = lax.dynamic_slice_in_dim(incoming, inside, block_width, 1)
        part_points = lax.dynamic_slice_in_dim(coordinates, inside, block_width, 1)
        kernel_table = maker(targets, part_points)
        return accumulated + lax.dot_general(
            part_density, kernel_table, (((1,), (1,)), ((), ())), preferred_element_type=jnp.float32
        )

    return lax.fori_loop(0, length // block_width, fold_one_block, running)


def build_table(targets, sources):
    source_count = sources.shape[1]
    block_width = math.gcd(source_count, 1024)
    table = jnp.zeros((targets.shape[1], source_count), jnp.bfloat16)

    def build_one_block(number, filled):
        inside = number * block_width
        part_points = lax.dynamic_slice_in_dim(sources, inside, block_width, 1)
        return lax.dynamic_update_slice_in_dim(
            filled, single_layer(targets, part_points), inside, 1
        )

    return lax.fori_loop(0, source_count // block_width, build_one_block, table)


def shared_shards(points, density, incident, precond, receivers):
    count_tgt = lax.axis_size("tgt")
    count_src = lax.axis_size("src")
    count_sub = lax.axis_size("sub")
    point_count = points.shape[1] * count_tgt * count_src * count_sub
    cell_area = FOUR_PI / point_count
    row_points = lax.all_gather(points, "src", axis=1, tiled=True)
    column_points = lax.all_gather(points, ("tgt", "sub"), axis=1, tiled=True)
    columns_count = density.shape[0]
    stored_table = build_table(row_points, column_points)
    for iteration in range(ITERS):
        weighted = (density * cell_area).astype(jnp.bfloat16)
        partial_sum = lax.dot_general(
            lax.all_gather(weighted, ("tgt", "sub"), axis=1, tiled=True),
            stored_table,
            (((1,), (1,)), ((), ())),
            preferred_element_type=jnp.float32,
        )
        field = lax.psum_scatter(partial_sum, "src", scatter_dimension=1, tiled=True)
        density = density - (field + incident) / precond[None, :]
    weighted = (density * cell_area).astype(jnp.bfloat16)
    receiver_blocks = receivers.reshape(count_tgt, count_src, count_sub, -1)
    picked = lax.dynamic_index_in_dim(receiver_blocks, lax.axis_index("tgt"), 0, keepdims=False)
    picked = lax.dynamic_index_in_dim(picked, lax.axis_index("sub"), 1, keepdims=False)
    toward = receiver_directions(picked.reshape(-1))
    empty_far = jnp.zeros((columns_count, toward.shape[1]), jnp.float32)
    far_partial = fold_blocks(
        empty_far,
        lax.all_gather(weighted, ("tgt", "sub"), axis=1, tiled=True),
        column_points,
        toward,
        far_kernel,
    )
    far_field = lax.psum_scatter(far_partial, "src", scatter_dimension=1, tiled=True)
    return (density, far_field)


def can_replicate(mesh, points):
    sizes = mesh.shape
    chips = sizes["tgt"] * sizes["src"]
    per_group = chips * sizes["sub"]
    total = points.shape[1] // sizes["groups"]
    return (
        sizes["sub"] == 2
        and chips >= 4
        and chips & (chips - 1) == 0
        and total == per_group * (BLOCK // 2)
        and total * total <= TABLE_LIMIT
    )


def solution(mesh):
    placed = (
        P(None, ("groups", "tgt", "src", "sub")),
        P(None, ("groups", "tgt", "src", "sub")),
        P(None, ("groups", "tgt", "src", "sub")),
        P(("groups", "tgt", "src", "sub")),
        P("groups"),
    )

    def whole(points, density, incident, precond, receivers):
        body = replicated_shards if can_replicate(mesh, points) else shared_shards
        return jax.shard_map(
            body,
            mesh=mesh,
            in_specs=placed,
            out_specs=(
                P(None, ("groups", "tgt", "src", "sub")),
                P(None, ("groups", "tgt", "src", "sub")),
            ),
            check_vma=False,
        )(points, density, incident, precond, receivers)

    return whole
```

```python
import functools
import math

import jax
import jax.numpy as jnp
from jax import lax
from jax.experimental import pallas as pl
from jax.experimental.pallas import tpu as pltpu
from jax.sharding import PartitionSpec as P

ITERS = 4
NDIR = 65536


WAVENUMBER = 32.0
SMOOTHING = 0.02
FOUR_PI = 4.0 * math.pi

TURNS = WAVENUMBER / (2.0 * math.pi)
SMOOTH_TURNS = (SMOOTHING * TURNS) ** 2
BLOCK = 256
UNROLL = 4
TABLE_LIMIT = 8 * 2**20
VMEM_LIMIT = 24 * 2**20


def sine_coefficients(count):
    nodes = [0.03125 + 0.03125 * math.cos(math.pi * (k + 0.5) / count) for k in range(count)]
    values = [math.sin(2.0 * math.pi * math.sqrt(u)) / math.sqrt(u) for u in nodes]
    divided = list(values)
    for level in range(1, count):
        for k in range(count - 1, level - 1, -1):
            divided[k] = (divided[k] - divided[k - 1]) / (nodes[k] - nodes[k - level])
    poly = [0.0] * count
    for k in range(count - 1, -1, -1):
        shifted = [0.0] + poly[:-1]
        poly = [s - nodes[k] * p for s, p in zip(shifted, poly)]
        poly[0] += divided[k]
    return poly


SINE = sine_coefficients(4)


def cos_turns(turns, scale):
    folded = 0.25 - jnp.abs(turns - jnp.round(turns))
    square = folded * folded
    value = SINE[-1] * scale
    for c in SINE[-2::-1]:
        value = value * square + c * scale
    return value * folded


def green(squared):
    kept = jnp.maximum(squared, 1e-12)
    turns = kept * lax.rsqrt(kept)
    return (cos_turns(turns, TURNS / FOUR_PI) * lax.rsqrt(squared + SMOOTH_TURNS)).astype(jnp.bfloat16)


def split3(x):
    high = x.astype(jnp.bfloat16).astype(jnp.float32)
    rest = x - high
    mid = rest.astype(jnp.bfloat16).astype(jnp.float32)
    low = (rest - mid).astype(jnp.bfloat16).astype(jnp.float32)
    return high, mid, low


def pack_kernel(points, precond, density, incident, receivers, out, picked, head, sems):
    columns = density.shape[0]
    chip = lax.axis_index("tgt") * lax.axis_size("src") + lax.axis_index("src")
    place = chip * lax.axis_size("sub") + lax.axis_index("sub")
    moves = [
        (points, head.at[0]),
        (precond, head.at[1, pl.ds(0, 1)]),
        (density, out.at[pl.ds(8, columns)]),
        (incident, out.at[pl.ds(8 + columns, columns)]),
        (receivers.at[pl.ds(place, 1)], picked),
    ]
    copies = [pltpu.make_async_copy(src, dst, sems.at[k]) for k, (src, dst) in enumerate(moves)]
    for copy in copies:
        copy.start()
    copies[0].wait()
    copies[1].wait()
    out[0:3, :] = head[0]
    out[3:4, :] = head[1, 0:1]
    out[4:8, :] = jnp.zeros((4, out.shape[1]), jnp.float32)
    for copy in copies[2:]:
        copy.wait()


def lanes(data, start, count):
    return jnp.concatenate(
        [piece[s, start : start + count, :] for piece in data for s in range(piece.shape[0])], axis=1
    )


def distance_operands(scaled):
    ones = jnp.ones((1, scaled.shape[1]), jnp.float32)
    left, right = [], []
    for k in range(3):
        h, m, l = split3(scaled[k : k + 1])
        left += [-2.0 * h, -2.0 * h, -2.0 * m, -2.0 * m, -2.0 * h, -2.0 * l]
        right += [h, m, h, m, l, h]
    norm = scaled[0:1] * scaled[0:1] + scaled[1:2] * scaled[1:2] + scaled[2:3] * scaled[2:3]
    h, m, l = split3(norm)
    left += [h, m, l, ones, ones, ones]
    right += [ones, ones, ones, h, m, l]
    zeros = jnp.zeros((8, scaled.shape[1]), jnp.float32)
    left = jnp.concatenate(left + [zeros], axis=0)
    right = jnp.concatenate(right + [zeros], axis=0).astype(jnp.bfloat16)
    return left.T.astype(jnp.bfloat16), right


def down(w, kernel_block):
    return lax.dot_general(w, kernel_block, (((1,), (0,)), ((), ())), preferred_element_type=jnp.float32)


def across(kernel_block, w):
    return lax.dot_general(kernel_block, w, (((1,), (1,)), ((), ())), preferred_element_type=jnp.float32)


def block_span(index):
    return pl.ds(pl.multiple_of(index * BLOCK, BLOCK), BLOCK)


def strip_size(old, new):
    return sum(j + 1 for j in range(old, old + new))


def build_strips(old, new, lhs, rhs, weighted, table, field, even, odd):
    count = strip_size(old, new)
    starts = [strip_size(old, k) for k in range(new)]

    def place(k):
        j, i = 0, k
        for step in range(1, new):
            past = k >= starts[step]
            j = jnp.where(past, step, j)
            i = jnp.where(past, k - starts[step], i)
        return j, i

    def distances(k):
        j, i = place(k)
        return lax.dot_general(
            lhs[block_span(j), :], rhs[:, block_span(i)], (((1,), (0,)), ((), ())), preferred_element_type=jnp.float32
        )

    def fill(k, source):
        for r in range(0, BLOCK, 32):
            table[k, r : r + 32, :] = green(source[r : r + 32, :])

    def products(k, valid=None):
        j, i = place(k)
        beside = jnp.where(old + j == i, 0.0, 1.0)
        above, below = weighted[:, block_span(i)], weighted[:, block_span(old + j)]
        if valid is not None:
            valid = jnp.where(valid, 1.0, 0.0)
            beside = beside * valid
            above = above * valid.astype(jnp.bfloat16)
        field[:, block_span(old + j)] += lax.dot_general(
            above, table[k], (((1,), (1,)), ((), ())), preferred_element_type=jnp.float32
        )
        field[:, block_span(i)] += down(below * beside.astype(jnp.bfloat16), table[k])

    field[...] = jnp.zeros_like(field)
    table[0] = jnp.zeros((BLOCK, BLOCK), jnp.bfloat16)
    stage = (even, odd)
    even[...] = distances(0)

    def several(t, carry):
        k = UNROLL * t
        for n in range(UNROLL):
            stage[(n + 1) % 2][...] = distances(jnp.minimum(k + n + 1, count - 1))
            if n == 0:
                products(jnp.maximum(k - 1, 0), k > 0)
            else:
                products(k + n - 1)
            fill(k + n, stage[n % 2])
        return carry

    lax.fori_loop(0, count // UNROLL, several, 0)
    for n, k in enumerate(range(count // UNROLL * UNROLL, count)):
        if k + 1 < count:
            stage[(n + 1) % 2][...] = distances(k + 1)
        if k:
            products(k - 1)
        fill(k, stage[n % 2])
    products(count - 1)


def prepare(old, data, columns, total, lhs, rhs, weighted, before):
    scaled = lanes(data, 0, 3) * TURNS
    left, right = distance_operands(scaled)
    lhs[...] = left
    rhs[:, old * BLOCK :] = right
    weighted[:, old * BLOCK :] = (lanes(data, 8, columns) * (FOUR_PI / total)).astype(jnp.bfloat16)
    if old:
        rhs[:, : old * BLOCK] = before[0][...]
        weighted[:, : old * BLOCK] = before[1][...]
    return scaled


def strips_kernel(pieces, old, new, columns, total, *refs):
    data, refs = refs[:pieces], refs[pieces:]
    before = refs[: 2 if old else 0]
    table, field, rhs, weighted, lhs, even, odd = refs[len(before) :]
    prepare(old, data, columns, total, lhs, rhs, weighted, before)
    build_strips(old, new, lhs, rhs, weighted, table, field, even, odd)


def iterate_kernel(pieces, new, blocks, columns, groups, *refs):
    data, refs = refs[:pieces], refs[pieces:]
    rest, refs = refs[:new], refs[new:]
    toward_ref, before, refs = refs[0], refs[1:3], refs[3:]
    tables, refs = refs[: len(groups)], refs[len(groups) :]
    fields, refs = refs[: len(groups)], refs[len(groups) :]
    density_out, far_out = refs[:2]
    lhs, rhs, weighted, table, field, even, odd, coords, plane, dens, inc = refs[2:]
    total = blocks * BLOCK
    width = data[0].shape[2]
    old = blocks - new
    prepare(old, rest, columns, total, lhs, rhs, weighted, before)
    build_strips(old, new, lhs, rhs, weighted, table, field, even, odd)

    everything = list(data) + list(rest)
    coords[0:3, :] = lanes(everything, 0, 3) * TURNS
    inverse = 1.0 / lanes(everything, 3, 1)
    dens[...] = lanes(everything, 8, columns)
    inc[...] = lanes(everything, 8 + columns, columns)
    for part in fields:
        field[:, : part.shape[1]] += part[...]
    dens[...] = dens[...] - (field[...] + inc[...]) * inverse

    entries = {}
    for (first, count), part in zip(list(groups) + [(old, new)], list(tables) + [table]):
        k = 0
        for j in range(first, first + count):
            for i in range(j + 1):
                entries[j, i] = (part, k)
                k += 1

    def entry(j, i):
        part, k = entries[j, i]
        return part[k]

    toward = toward_ref[...].T
    cell_area = FOUR_PI / total

    def rounded():
        return (dens[...] * cell_area).astype(jnp.bfloat16)

    def part_of(w, b):
        return w[:, b * BLOCK : (b + 1) * BLOCK]

    steps = ITERS - 1
    per_step = -(-blocks // steps)

    def iterate(step, carry):
        w = rounded()
        for k in range(per_step):
            span = block_span(jnp.minimum(step * per_step + k, blocks - 1))
            phase = toward[:, 0:1] * coords[0:1, span] + toward[:, 1:2] * coords[1:2, span]
            phase = phase + toward[:, 2:3] * coords[2:3, span]
            plane[:, span] = cos_turns(phase, 1.0).astype(jnp.bfloat16)
        downs, sides = [None] * blocks, [None] * blocks
        for b in range(blocks):
            top = blocks - 1 - b
            for n in range(max(blocks - b, top)):
                if b + n < blocks:
                    term = down(part_of(w, b + n), entry(b + n, b))
                    downs[b] = term if n == 0 else downs[b] + term
                if n < top:
                    term = across(entry(top, n), part_of(w, n))
                    sides[top] = term if n == 0 else sides[top] + term
        for b in range(blocks):
            total_field = downs[b] if sides[b] is None else downs[b] + sides[b].T
            span = slice(b * BLOCK, (b + 1) * BLOCK)
            dens[:, span] = dens[:, span] - (total_field + inc[:, span]) * inverse[:, span]
        return carry

    lax.fori_loop(0, steps, iterate, 0)
    density_out[...] = dens[:, 0:width]
    far_out[...] = across(plane[...], rounded()).T


def replicated_shards(points, density, incident, precond, receivers):
    count_tgt = lax.axis_size("tgt")
    count_src = lax.axis_size("src")
    count_sub = lax.axis_size("sub")
    chips = count_tgt * count_src
    columns, width = density.shape
    names = ("tgt", "src", "sub")
    vmem = pl.BlockSpec(memory_space=pltpu.VMEM)
    rows = receivers.shape[0] // (chips * count_sub)
    inputs = (points, precond[None, :], density, incident, receivers.reshape(-1, rows))
    payload, picked = pl.pallas_call(
        pack_kernel,
        out_shape=(
            jax.ShapeDtypeStruct((8 + 2 * columns, width), jnp.float32),
            jax.ShapeDtypeStruct((1, rows), jnp.int32),
        ),
        in_specs=[pl.BlockSpec(memory_space=pltpu.HBM)] * len(inputs),
        out_specs=(vmem, vmem),
        scratch_shapes=[pltpu.VMEM((2, 3, width), jnp.float32), pltpu.SemaphoreType.DMA((len(inputs),))],
        compiler_params=pltpu.CompilerParams(vmem_limit_bytes=4 * 2**20),
        name="pack",
    )(*(pltpu.with_memory_space_constraint(array, pltpu.HBM) for array in inputs))
    swap = [(0, 1), (1, 0)]
    payload = payload[None]

    def fetch(array, offsets):
        pairs = [(q * 2 + c, (q ^ offsets[c]) * 2 + c) for q in range(chips) for c in range(2)]
        return lax.ppermute(array, names, pairs)

    far = fetch(payload, (chips - 1, chips - 1))
    own = jnp.concatenate([payload, lax.ppermute(payload, "sub", swap)], axis=0)
    near = [fetch(own, (k, k + 1)) for k in range(1, chips - 1, 2)]

    toward = receiver_directions(picked[0])
    toward = jnp.concatenate([toward, jnp.zeros((5, rows), jnp.float32)], axis=0)

    blocks = chips
    total = blocks * BLOCK
    f32, bf16 = jnp.float32, jnp.bfloat16

    def strip_shapes(old, new):
        return [
            ((strip_size(old, new), BLOCK, BLOCK), bf16),
            ((columns, (old + new) * BLOCK), f32),
            ((32, (old + new) * BLOCK), bf16),
            ((columns, (old + new) * BLOCK), bf16),
            ((new * BLOCK, 32), bf16),
            ((BLOCK, BLOCK), f32),
            ((BLOCK, BLOCK), f32),
        ]

    groups, tables, fields, held, before = [], [], [], [], []

    def strips(data):
        old, new = (sum(array.shape[0] for array in arrays) // 2 for arrays in (held, data))
        shapes = strip_shapes(old, new)
        work = strip_size(old, new) * BLOCK * BLOCK
        table, field, *state = pl.pallas_call(
            functools.partial(strips_kernel, len(data), old, new, columns, total),
            out_shape=[jax.ShapeDtypeStruct(*shape) for shape in shapes[:4]],
            in_specs=[vmem] * (len(data) + len(before)),
            out_specs=[vmem] * 4,
            scratch_shapes=[pltpu.VMEM(*shape) for shape in shapes[4:]],
            compiler_params=pltpu.CompilerParams(vmem_limit_bytes=VMEM_LIMIT),
            cost_estimate=pl.CostEstimate(flops=30 * work, bytes_accessed=2 * work, transcendentals=2 * work),
            name=f"strips{old}",
        )(*data, *before)
        groups.append((old, new))
        tables.append(table)
        fields.append(field)
        held.extend(data)
        before[:] = state

    def both(array):
        return [array, lax.ppermute(array, "sub", swap)]

    def swapped(array):
        return lax.ppermute(array, "sub", swap)

    first, late = [own, far, swapped(far)], near
    if len(near) > 1:
        first[1:1] = [near[0], swapped(near[0])]
        late = near[1:]
    strips(first)
    *late, fields[0] = lax.optimization_barrier((*late, fields[0]))
    rest = [swapped(array) for array in late]
    strips(late)
    pieces, new = len(held), len(rest)
    shapes = strip_shapes(blocks - new, new)
    return pl.pallas_call(
        functools.partial(iterate_kernel, pieces, new, blocks, columns, tuple(groups)),
        out_shape=(
            jax.ShapeDtypeStruct((columns, width), f32),
            jax.ShapeDtypeStruct((columns, rows), f32),
        ),
        in_specs=[vmem] * (pieces + new + 3 + 2 * len(groups)),
        out_specs=(vmem, vmem),
        scratch_shapes=[pltpu.VMEM(*shapes[k]) for k in (4, 2, 3, 0, 1, 5, 6)]
        + [
            pltpu.VMEM((8, total), f32),
            pltpu.VMEM((rows, total), bf16),
            pltpu.VMEM((columns, total), f32),
            pltpu.VMEM((columns, total), f32),
        ],
        compiler_params=pltpu.CompilerParams(vmem_limit_bytes=VMEM_LIMIT),
        name="iterate",
    )(*held, *rest, toward, *before, *tables, *fields)


def single_layer(targets, sources):
    delta_x = targets[0][:, None] - sources[0][None, :]
    delta_y = targets[1][:, None] - sources[1][None, :]
    delta_z = targets[2][:, None] - sources[2][None, :]
    squared = delta_x * delta_x + delta_y * delta_y + delta_z * delta_z
    values = jnp.cos(WAVENUMBER * jnp.sqrt(squared)) / (
        FOUR_PI * jnp.sqrt(squared + SMOOTHING * SMOOTHING)
    )
    return values.astype(jnp.bfloat16)


def far_kernel(toward, sources):
    projection = toward[0][:, None] * sources[0][None, :] + toward[1][:, None] * sources[1][None, :]
    projection = projection + toward[2][:, None] * sources[2][None, :]
    return jnp.cos(WAVENUMBER * projection).astype(jnp.bfloat16)


def receiver_directions(direction_index):
    upper_part = direction_index // 256
    lower_part = direction_index % 256
    rotation = (upper_part * 14080 + lower_part * 40503) % 65536
    azimuth = rotation.astype(jnp.float32) * (2.0 * math.pi / 65536.0)
    height = 1.0 - (2 * direction_index + 1).astype(jnp.float32) / NDIR
    radial = jnp.sqrt(jnp.maximum(1.0 - height * height, 0.0))
    return jnp.stack([radial * jnp.cos(azimuth), radial * jnp.sin(azimuth), height])


def fold_blocks(running, incoming, coordinates, targets, maker):
    length = incoming.shape[1]
    block_width = math.gcd(length, 1024)

    def fold_one_block(number, accumulated):
        inside = number * block_width
        part_density = lax.dynamic_slice_in_dim(incoming, inside, block_width, 1)
        part_points = lax.dynamic_slice_in_dim(coordinates, inside, block_width, 1)
        kernel_table = maker(targets, part_points)
        return accumulated + lax.dot_general(
            part_density, kernel_table, (((1,), (1,)), ((), ())), preferred_element_type=jnp.float32
        )

    return lax.fori_loop(0, length // block_width, fold_one_block, running)


def build_table(targets, sources):
    source_count = sources.shape[1]
    block_width = math.gcd(source_count, 1024)
    table = jnp.zeros((targets.shape[1], source_count), jnp.bfloat16)

    def build_one_block(number, filled):
        inside = number * block_width
        part_points = lax.dynamic_slice_in_dim(sources, inside, block_width, 1)
        return lax.dynamic_update_slice_in_dim(
            filled, single_layer(targets, part_points), inside, 1
        )

    return lax.fori_loop(0, source_count // block_width, build_one_block, table)


def shared_shards(points, density, incident, precond, receivers):
    count_tgt = lax.axis_size("tgt")
    count_src = lax.axis_size("src")
    count_sub = lax.axis_size("sub")
    point_count = points.shape[1] * count_tgt * count_src * count_sub
    cell_area = FOUR_PI / point_count
    row_points = lax.all_gather(points, "src", axis=1, tiled=True)
    column_points = lax.all_gather(points, ("tgt", "sub"), axis=1, tiled=True)
    columns_count = density.shape[0]
    stored_table = build_table(row_points, column_points)
    for iteration in range(ITERS):
        weighted = (density * cell_area).astype(jnp.bfloat16)
        partial_sum = lax.dot_general(
            lax.all_gather(weighted, ("tgt", "sub"), axis=1, tiled=True),
            stored_table,
            (((1,), (1,)), ((), ())),
            preferred_element_type=jnp.float32,
        )
        field = lax.psum_scatter(partial_sum, "src", scatter_dimension=1, tiled=True)
        density = density - (field + incident) / precond[None, :]
    weighted = (density * cell_area).astype(jnp.bfloat16)
    receiver_blocks = receivers.reshape(count_tgt, count_src, count_sub, -1)
    picked = lax.dynamic_index_in_dim(receiver_blocks, lax.axis_index("tgt"), 0, keepdims=False)
    picked = lax.dynamic_index_in_dim(picked, lax.axis_index("sub"), 1, keepdims=False)
    toward = receiver_directions(picked.reshape(-1))
    empty_far = jnp.zeros((columns_count, toward.shape[1]), jnp.float32)
    far_partial = fold_blocks(
        empty_far,
        lax.all_gather(weighted, ("tgt", "sub"), axis=1, tiled=True),
        column_points,
        toward,
        far_kernel,
    )
    far_field = lax.psum_scatter(far_partial, "src", scatter_dimension=1, tiled=True)
    return (density, far_field)


def can_replicate(mesh, points):
    sizes = mesh.shape
    chips = sizes["tgt"] * sizes["src"]
    per_group = chips * sizes["sub"]
    total = points.shape[1] // sizes["groups"]
    return (
        sizes["sub"] == 2
        and chips >= 4
        and chips & (chips - 1) == 0
        and total == per_group * (BLOCK // 2)
        and total * total <= TABLE_LIMIT
    )


def solution(mesh):
    placed = (
        P(None, ("groups", "tgt", "src", "sub")),
        P(None, ("groups", "tgt", "src", "sub")),
        P(None, ("groups", "tgt", "src", "sub")),
        P(("groups", "tgt", "src", "sub")),
        P("groups"),
    )

    def whole(points, density, incident, precond, receivers):
        body = replicated_shards if can_replicate(mesh, points) else shared_shards
        return jax.shard_map(
            body,
            mesh=mesh,
            in_specs=placed,
            out_specs=(
                P(None, ("groups", "tgt", "src", "sub")),
                P(None, ("groups", "tgt", "src", "sub")),
            ),
            check_vma=False,
        )(points, density, incident, precond, receivers)

    return whole
```

```python
import functools
import math

import jax
import jax.numpy as jnp
from jax import lax
from jax.experimental import pallas as pl
from jax.experimental.pallas import tpu as pltpu
from jax.sharding import PartitionSpec as P

ITERS = 4
NDIR = 65536


WAVENUMBER = 32.0
SMOOTHING = 0.02
FOUR_PI = 4.0 * math.pi

TURNS = WAVENUMBER / (2.0 * math.pi)
SMOOTH_TURNS = (SMOOTHING * TURNS) ** 2
BLOCK = 256
UNROLL = 8
TABLE_LIMIT = 8 * 2**20
VMEM_LIMIT = 24 * 2**20


def sine_coefficients(count):
    nodes = [0.03125 + 0.03125 * math.cos(math.pi * (k + 0.5) / count) for k in range(count)]
    values = [math.sin(2.0 * math.pi * math.sqrt(u)) / math.sqrt(u) for u in nodes]
    divided = list(values)
    for level in range(1, count):
        for k in range(count - 1, level - 1, -1):
            divided[k] = (divided[k] - divided[k - 1]) / (nodes[k] - nodes[k - level])
    poly = [0.0] * count
    for k in range(count - 1, -1, -1):
        shifted = [0.0] + poly[:-1]
        poly = [s - nodes[k] * p for s, p in zip(shifted, poly)]
        poly[0] += divided[k]
    return poly


SINE = sine_coefficients(4)


def cos_turns(turns, scale):
    folded = 0.25 - jnp.abs(turns - jnp.round(turns))
    square = folded * folded
    value = SINE[-1] * scale
    for c in SINE[-2::-1]:
        value = value * square + c * scale
    return value * folded


def green(squared):
    kept = jnp.maximum(squared, 1e-12)
    turns = kept * lax.rsqrt(kept)
    return (cos_turns(turns, TURNS / FOUR_PI) * lax.rsqrt(squared + SMOOTH_TURNS)).astype(jnp.bfloat16)


def split3(x):
    high = x.astype(jnp.bfloat16).astype(jnp.float32)
    rest = x - high
    mid = rest.astype(jnp.bfloat16).astype(jnp.float32)
    low = (rest - mid).astype(jnp.bfloat16).astype(jnp.float32)
    return high, mid, low


def pack_kernel(points, precond, density, incident, receivers, out, picked, head, sems):
    columns = density.shape[0]
    chip = lax.axis_index("tgt") * lax.axis_size("src") + lax.axis_index("src")
    place = chip * lax.axis_size("sub") + lax.axis_index("sub")
    moves = [
        (points, head.at[0]),
        (precond, head.at[1, pl.ds(0, 1)]),
        (density, out.at[pl.ds(8, columns)]),
        (incident, out.at[pl.ds(8 + columns, columns)]),
        (receivers.at[pl.ds(place, 1)], picked),
    ]
    copies = [pltpu.make_async_copy(src, dst, sems.at[k]) for k, (src, dst) in enumerate(moves)]
    for copy in copies:
        copy.start()
    copies[0].wait()
    copies[1].wait()
    out[0:3, :] = head[0]
    out[3:4, :] = head[1, 0:1]
    out[4:8, :] = jnp.zeros((4, out.shape[1]), jnp.float32)
    for copy in copies[2:]:
        copy.wait()


def lanes(data, start, count):
    return jnp.concatenate(
        [piece[s, start : start + count, :] for piece in data for s in range(piece.shape[0])], axis=1
    )


def distance_operands(scaled):
    ones = jnp.ones((1, scaled.shape[1]), jnp.float32)
    left, right = [], []
    for k in range(3):
        h, m, l = split3(scaled[k : k + 1])
        left += [-2.0 * h, -2.0 * h, -2.0 * m, -2.0 * m, -2.0 * h, -2.0 * l]
        right += [h, m, h, m, l, h]
    norm = scaled[0:1] * scaled[0:1] + scaled[1:2] * scaled[1:2] + scaled[2:3] * scaled[2:3]
    h, m, l = split3(norm)
    left += [h, m, l, ones, ones, ones]
    right += [ones, ones, ones, h, m, l]
    zeros = jnp.zeros((8, scaled.shape[1]), jnp.float32)
    left = jnp.concatenate(left + [zeros], axis=0)
    right = jnp.concatenate(right + [zeros], axis=0).astype(jnp.bfloat16)
    return left.T.astype(jnp.bfloat16), right


def down(w, kernel_block):
    return lax.dot_general(w, kernel_block, (((1,), (0,)), ((), ())), preferred_element_type=jnp.float32)


def across(kernel_block, w):
    return lax.dot_general(kernel_block, w, (((1,), (1,)), ((), ())), preferred_element_type=jnp.float32)


def block_span(index):
    return pl.ds(pl.multiple_of(index * BLOCK, BLOCK), BLOCK)


def strip_size(old, new):
    return sum(j + 1 for j in range(old, old + new))


def build_strips(old, new, lhs, rhs, weighted, table, field, even, odd):
    count = strip_size(old, new)
    starts = [strip_size(old, k) for k in range(new)]

    def place(k):
        j, i = 0, k
        for step in range(1, new):
            past = k >= starts[step]
            j = jnp.where(past, step, j)
            i = jnp.where(past, k - starts[step], i)
        return j, i

    def distances(k):
        j, i = place(k)
        return lax.dot_general(
            lhs[block_span(j), :], rhs[:, block_span(i)], (((1,), (0,)), ((), ())), preferred_element_type=jnp.float32
        )

    def fill(k, source):
        for r in range(0, BLOCK, 32):
            table[k, r : r + 32, :] = green(source[r : r + 32, :])

    def products(k, valid=None):
        j, i = place(k)
        beside = jnp.where(old + j == i, 0.0, 1.0)
        above, below = weighted[:, block_span(i)], weighted[:, block_span(old + j)]
        if valid is not None:
            valid = jnp.where(valid, 1.0, 0.0)
            beside = beside * valid
            above = above * valid.astype(jnp.bfloat16)
        field[:, block_span(old + j)] += lax.dot_general(
            above, table[k], (((1,), (1,)), ((), ())), preferred_element_type=jnp.float32
        )
        field[:, block_span(i)] += down(below * beside.astype(jnp.bfloat16), table[k])

    field[...] = jnp.zeros_like(field)
    table[0] = jnp.zeros((BLOCK, BLOCK), jnp.bfloat16)
    stage = (even, odd)
    even[...] = distances(0)

    def several(t, carry):
        k = UNROLL * t
        for n in range(UNROLL):
            stage[(n + 1) % 2][...] = distances(jnp.minimum(k + n + 1, count - 1))
            if n == 0:
                products(jnp.maximum(k - 1, 0), k > 0)
            else:
                products(k + n - 1)
            fill(k + n, stage[n % 2])
        return carry

    lax.fori_loop(0, count // UNROLL, several, 0)
    for n, k in enumerate(range(count // UNROLL * UNROLL, count)):
        if k + 1 < count:
            stage[(n + 1) % 2][...] = distances(k + 1)
        if k:
            products(k - 1)
        fill(k, stage[n % 2])
    products(count - 1)


def prepare(old, data, columns, total, lhs, rhs, weighted, before):
    scaled = lanes(data, 0, 3) * TURNS
    left, right = distance_operands(scaled)
    lhs[...] = left
    rhs[:, old * BLOCK :] = right
    weighted[:, old * BLOCK :] = (lanes(data, 8, columns) * (FOUR_PI / total)).astype(jnp.bfloat16)
    if old:
        rhs[:, : old * BLOCK] = before[0][...]
        weighted[:, : old * BLOCK] = before[1][...]
    return scaled


def strips_kernel(pieces, old, new, columns, total, *refs):
    data, refs = refs[:pieces], refs[pieces:]
    before = refs[: 2 if old else 0]
    table, field, rhs, weighted, lhs, even, odd = refs[len(before) :]
    prepare(old, data, columns, total, lhs, rhs, weighted, before)
    build_strips(old, new, lhs, rhs, weighted, table, field, even, odd)


def iterate_kernel(pieces, new, blocks, columns, groups, *refs):
    data, refs = refs[:pieces], refs[pieces:]
    rest, refs = refs[:new], refs[new:]
    toward_ref, before, refs = refs[0], refs[1:3], refs[3:]
    tables, refs = refs[: len(groups)], refs[len(groups) :]
    fields, refs = refs[: len(groups)], refs[len(groups) :]
    density_out, far_out = refs[:2]
    lhs, rhs, weighted, table, field, even, odd, coords, plane, dens, inc = refs[2:]
    total = blocks * BLOCK
    width = data[0].shape[2]
    old = blocks - new
    prepare(old, rest, columns, total, lhs, rhs, weighted, before)
    build_strips(old, new, lhs, rhs, weighted, table, field, even, odd)

    everything = list(data) + list(rest)
    coords[0:3, :] = lanes(everything, 0, 3) * TURNS
    inverse = 1.0 / lanes(everything, 3, 1)
    dens[...] = lanes(everything, 8, columns)
    inc[...] = lanes(everything, 8 + columns, columns)
    for part in fields:
        field[:, : part.shape[1]] += part[...]
    dens[...] = dens[...] - (field[...] + inc[...]) * inverse

    entries = {}
    for (first, count), part in zip(list(groups) + [(old, new)], list(tables) + [table]):
        k = 0
        for j in range(first, first + count):
            for i in range(j + 1):
                entries[j, i] = (part, k)
                k += 1

    def entry(j, i):
        part, k = entries[j, i]
        return part[k]

    toward = toward_ref[...].T
    cell_area = FOUR_PI / total

    def rounded():
        return (dens[...] * cell_area).astype(jnp.bfloat16)

    def part_of(w, b):
        return w[:, b * BLOCK : (b + 1) * BLOCK]

    steps = ITERS - 1
    per_step = -(-blocks // steps)

    def iterate(step, carry):
        w = rounded()
        for k in range(per_step):
            span = block_span(jnp.minimum(step * per_step + k, blocks - 1))
            phase = toward[:, 0:1] * coords[0:1, span] + toward[:, 1:2] * coords[1:2, span]
            phase = phase + toward[:, 2:3] * coords[2:3, span]
            plane[:, span] = cos_turns(phase, 1.0).astype(jnp.bfloat16)
        downs, sides = [None] * blocks, [None] * blocks
        for b in range(blocks):
            top = blocks - 1 - b
            for n in range(max(blocks - b, top)):
                if b + n < blocks:
                    term = down(part_of(w, b + n), entry(b + n, b))
                    downs[b] = term if n == 0 else downs[b] + term
                if n < top:
                    term = across(entry(top, n), part_of(w, n))
                    sides[top] = term if n == 0 else sides[top] + term
        for b in range(blocks):
            total_field = downs[b] if sides[b] is None else downs[b] + sides[b].T
            span = slice(b * BLOCK, (b + 1) * BLOCK)
            dens[:, span] = dens[:, span] - (total_field + inc[:, span]) * inverse[:, span]
        return carry

    lax.fori_loop(0, steps, iterate, 0)
    density_out[...] = dens[:, 0:width]
    far_out[...] = across(rounded(), plane[...])


def replicated_shards(points, density, incident, precond, receivers):
    count_tgt = lax.axis_size("tgt")
    count_src = lax.axis_size("src")
    count_sub = lax.axis_size("sub")
    chips = count_tgt * count_src
    columns, width = density.shape
    names = ("tgt", "src", "sub")
    vmem = pl.BlockSpec(memory_space=pltpu.VMEM)
    rows = receivers.shape[0] // (chips * count_sub)
    inputs = (points, precond[None, :], density, incident, receivers.reshape(-1, rows))
    payload, picked = pl.pallas_call(
        pack_kernel,
        out_shape=(
            jax.ShapeDtypeStruct((8 + 2 * columns, width), jnp.float32),
            jax.ShapeDtypeStruct((1, rows), jnp.int32),
        ),
        in_specs=[pl.BlockSpec(memory_space=pltpu.HBM)] * len(inputs),
        out_specs=(vmem, vmem),
        scratch_shapes=[pltpu.VMEM((2, 3, width), jnp.float32), pltpu.SemaphoreType.DMA((len(inputs),))],
        compiler_params=pltpu.CompilerParams(vmem_limit_bytes=4 * 2**20),
        name="pack",
    )(*(pltpu.with_memory_space_constraint(array, pltpu.HBM) for array in inputs))
    swap = [(0, 1), (1, 0)]
    payload = payload[None]

    def fetch(array, offsets):
        pairs = [(q * 2 + c, (q ^ offsets[c]) * 2 + c) for q in range(chips) for c in range(2)]
        return lax.ppermute(array, names, pairs)

    far = fetch(payload, (chips - 1, chips - 1))
    own = jnp.concatenate([payload, lax.ppermute(payload, "sub", swap)], axis=0)
    near = [fetch(own, (k, k + 1)) for k in range(1, chips - 1, 2)]

    toward = receiver_directions(picked[0])
    toward = jnp.concatenate([toward, jnp.zeros((5, rows), jnp.float32)], axis=0)

    blocks = chips
    total = blocks * BLOCK
    f32, bf16 = jnp.float32, jnp.bfloat16

    def strip_shapes(old, new):
        return [
            ((strip_size(old, new), BLOCK, BLOCK), bf16),
            ((columns, (old + new) * BLOCK), f32),
            ((32, (old + new) * BLOCK), bf16),
            ((columns, (old + new) * BLOCK), bf16),
            ((new * BLOCK, 32), bf16),
            ((BLOCK, BLOCK), f32),
            ((BLOCK, BLOCK), f32),
        ]

    groups, tables, fields, held, before = [], [], [], [], []

    def strips(data):
        old, new = (sum(array.shape[0] for array in arrays) // 2 for arrays in (held, data))
        shapes = strip_shapes(old, new)
        work = strip_size(old, new) * BLOCK * BLOCK
        table, field, *state = pl.pallas_call(
            functools.partial(strips_kernel, len(data), old, new, columns, total),
            out_shape=[jax.ShapeDtypeStruct(*shape) for shape in shapes[:4]],
            in_specs=[vmem] * (len(data) + len(before)),
            out_specs=[vmem] * 4,
            scratch_shapes=[pltpu.VMEM(*shape) for shape in shapes[4:]],
            compiler_params=pltpu.CompilerParams(vmem_limit_bytes=VMEM_LIMIT),
            cost_estimate=pl.CostEstimate(flops=30 * work, bytes_accessed=2 * work, transcendentals=2 * work),
            name=f"strips{old}",
        )(*data, *before)
        groups.append((old, new))
        tables.append(table)
        fields.append(field)
        held.extend(data)
        before[:] = state

    def both(array):
        return [array, lax.ppermute(array, "sub", swap)]

    def swapped(array):
        return lax.ppermute(array, "sub", swap)

    first, late = [own, far, swapped(far)], near
    if len(near) > 1:
        first[1:1] = [near[0], swapped(near[0])]
        late = near[1:]
    strips(first)
    *late, fields[0] = lax.optimization_barrier((*late, fields[0]))
    rest = [swapped(array) for array in late]
    strips(late)
    pieces, new = len(held), len(rest)
    shapes = strip_shapes(blocks - new, new)
    return pl.pallas_call(
        functools.partial(iterate_kernel, pieces, new, blocks, columns, tuple(groups)),
        out_shape=(
            jax.ShapeDtypeStruct((columns, width), f32),
            jax.ShapeDtypeStruct((columns, rows), f32),
        ),
        in_specs=[vmem] * (pieces + new + 3 + 2 * len(groups)),
        out_specs=(vmem, vmem),
        scratch_shapes=[pltpu.VMEM(*shapes[k]) for k in (4, 2, 3, 0, 1, 5, 6)]
        + [
            pltpu.VMEM((8, total), f32),
            pltpu.VMEM((rows, total), bf16),
            pltpu.VMEM((columns, total), f32),
            pltpu.VMEM((columns, total), f32),
        ],
        compiler_params=pltpu.CompilerParams(vmem_limit_bytes=VMEM_LIMIT),
        name="iterate",
    )(*held, *rest, toward, *before, *tables, *fields)


def single_layer(targets, sources):
    delta_x = targets[0][:, None] - sources[0][None, :]
    delta_y = targets[1][:, None] - sources[1][None, :]
    delta_z = targets[2][:, None] - sources[2][None, :]
    squared = delta_x * delta_x + delta_y * delta_y + delta_z * delta_z
    values = jnp.cos(WAVENUMBER * jnp.sqrt(squared)) / (
        FOUR_PI * jnp.sqrt(squared + SMOOTHING * SMOOTHING)
    )
    return values.astype(jnp.bfloat16)


def far_kernel(toward, sources):
    projection = toward[0][:, None] * sources[0][None, :] + toward[1][:, None] * sources[1][None, :]
    projection = projection + toward[2][:, None] * sources[2][None, :]
    return jnp.cos(WAVENUMBER * projection).astype(jnp.bfloat16)


def receiver_directions(direction_index):
    upper_part = direction_index // 256
    lower_part = direction_index % 256
    rotation = (upper_part * 14080 + lower_part * 40503) % 65536
    azimuth = rotation.astype(jnp.float32) * (2.0 * math.pi / 65536.0)
    height = 1.0 - (2 * direction_index + 1).astype(jnp.float32) / NDIR
    radial = jnp.sqrt(jnp.maximum(1.0 - height * height, 0.0))
    return jnp.stack([radial * jnp.cos(azimuth), radial * jnp.sin(azimuth), height])


def fold_blocks(running, incoming, coordinates, targets, maker):
    length = incoming.shape[1]
    block_width = math.gcd(length, 1024)

    def fold_one_block(number, accumulated):
        inside = number * block_width
        part_density = lax.dynamic_slice_in_dim(incoming, inside, block_width, 1)
        part_points = lax.dynamic_slice_in_dim(coordinates, inside, block_width, 1)
        kernel_table = maker(targets, part_points)
        return accumulated + lax.dot_general(
            part_density, kernel_table, (((1,), (1,)), ((), ())), preferred_element_type=jnp.float32
        )

    return lax.fori_loop(0, length // block_width, fold_one_block, running)


def build_table(targets, sources):
    source_count = sources.shape[1]
    block_width = math.gcd(source_count, 1024)
    table = jnp.zeros((targets.shape[1], source_count), jnp.bfloat16)

    def build_one_block(number, filled):
        inside = number * block_width
        part_points = lax.dynamic_slice_in_dim(sources, inside, block_width, 1)
        return lax.dynamic_update_slice_in_dim(
            filled, single_layer(targets, part_points), inside, 1
        )

    return lax.fori_loop(0, source_count // block_width, build_one_block, table)


def shared_shards(points, density, incident, precond, receivers):
    count_tgt = lax.axis_size("tgt")
    count_src = lax.axis_size("src")
    count_sub = lax.axis_size("sub")
    point_count = points.shape[1] * count_tgt * count_src * count_sub
    cell_area = FOUR_PI / point_count
    row_points = lax.all_gather(points, "src", axis=1, tiled=True)
    column_points = lax.all_gather(points, ("tgt", "sub"), axis=1, tiled=True)
    columns_count = density.shape[0]
    stored_table = build_table(row_points, column_points)
    for iteration in range(ITERS):
        weighted = (density * cell_area).astype(jnp.bfloat16)
        partial_sum = lax.dot_general(
            lax.all_gather(weighted, ("tgt", "sub"), axis=1, tiled=True),
            stored_table,
            (((1,), (1,)), ((), ())),
            preferred_element_type=jnp.float32,
        )
        field = lax.psum_scatter(partial_sum, "src", scatter_dimension=1, tiled=True)
        density = density - (field + incident) / precond[None, :]
    weighted = (density * cell_area).astype(jnp.bfloat16)
    receiver_blocks = receivers.reshape(count_tgt, count_src, count_sub, -1)
    picked = lax.dynamic_index_in_dim(receiver_blocks, lax.axis_index("tgt"), 0, keepdims=False)
    picked = lax.dynamic_index_in_dim(picked, lax.axis_index("sub"), 1, keepdims=False)
    toward = receiver_directions(picked.reshape(-1))
    empty_far = jnp.zeros((columns_count, toward.shape[1]), jnp.float32)
    far_partial = fold_blocks(
        empty_far,
        lax.all_gather(weighted, ("tgt", "sub"), axis=1, tiled=True),
        column_points,
        toward,
        far_kernel,
    )
    far_field = lax.psum_scatter(far_partial, "src", scatter_dimension=1, tiled=True)
    return (density, far_field)


def can_replicate(mesh, points):
    sizes = mesh.shape
    chips = sizes["tgt"] * sizes["src"]
    per_group = chips * sizes["sub"]
    total = points.shape[1] // sizes["groups"]
    return (
        sizes["sub"] == 2
        and chips >= 4
        and chips & (chips - 1) == 0
        and total == per_group * (BLOCK // 2)
        and total * total <= TABLE_LIMIT
    )


def solution(mesh):
    placed = (
        P(None, ("groups", "tgt", "src", "sub")),
        P(None, ("groups", "tgt", "src", "sub")),
        P(None, ("groups", "tgt", "src", "sub")),
        P(("groups", "tgt", "src", "sub")),
        P("groups"),
    )

    def whole(points, density, incident, precond, receivers):
        body = replicated_shards if can_replicate(mesh, points) else shared_shards
        return jax.shard_map(
            body,
            mesh=mesh,
            in_specs=placed,
            out_specs=(
                P(None, ("groups", "tgt", "src", "sub")),
                P(None, ("groups", "tgt", "src", "sub")),
            ),
            check_vma=False,
        )(points, density, incident, precond, receivers)

    return whole
```

```python
import functools
import math

import jax
import jax.numpy as jnp
from jax import lax
from jax.experimental import pallas as pl
from jax.experimental.pallas import tpu as pltpu
from jax.sharding import PartitionSpec as P

ITERS = 4
NDIR = 65536


WAVENUMBER = 32.0
SMOOTHING = 0.02
FOUR_PI = 4.0 * math.pi

TURNS = WAVENUMBER / (2.0 * math.pi)
SMOOTH_TURNS = (SMOOTHING * TURNS) ** 2
BLOCK = 256
UNROLL = 8
TABLE_LIMIT = 8 * 2**20
VMEM_LIMIT = 24 * 2**20


def sine_coefficients(count):
    nodes = [0.03125 + 0.03125 * math.cos(math.pi * (k + 0.5) / count) for k in range(count)]
    values = [math.sin(2.0 * math.pi * math.sqrt(u)) / math.sqrt(u) for u in nodes]
    divided = list(values)
    for level in range(1, count):
        for k in range(count - 1, level - 1, -1):
            divided[k] = (divided[k] - divided[k - 1]) / (nodes[k] - nodes[k - level])
    poly = [0.0] * count
    for k in range(count - 1, -1, -1):
        shifted = [0.0] + poly[:-1]
        poly = [s - nodes[k] * p for s, p in zip(shifted, poly)]
        poly[0] += divided[k]
    return poly


SINE = sine_coefficients(4)


def cos_turns(turns, scale):
    folded = 0.25 - jnp.abs(turns - jnp.round(turns))
    square = folded * folded
    value = SINE[-1] * scale
    for c in SINE[-2::-1]:
        value = value * square + c * scale
    return value * folded


def green(squared):
    kept = jnp.maximum(squared, 1e-12)
    turns = kept * lax.rsqrt(kept)
    return (cos_turns(turns, TURNS / FOUR_PI) * lax.rsqrt(squared + SMOOTH_TURNS)).astype(jnp.bfloat16)


def split3(x):
    high = x.astype(jnp.bfloat16).astype(jnp.float32)
    rest = x - high
    mid = rest.astype(jnp.bfloat16).astype(jnp.float32)
    low = (rest - mid).astype(jnp.bfloat16).astype(jnp.float32)
    return high, mid, low


def pack_kernel(points, precond, density, incident, receivers, out, picked, head, sems):
    columns = density.shape[0]
    chip = lax.axis_index("tgt") * lax.axis_size("src") + lax.axis_index("src")
    place = chip * lax.axis_size("sub") + lax.axis_index("sub")
    moves = [
        (points, head.at[0]),
        (precond, head.at[1, pl.ds(0, 1)]),
        (density, out.at[pl.ds(8, columns)]),
        (incident, out.at[pl.ds(8 + columns, columns)]),
        (receivers.at[pl.ds(place, 1)], picked),
    ]
    copies = [pltpu.make_async_copy(src, dst, sems.at[k]) for k, (src, dst) in enumerate(moves)]
    for copy in copies:
        copy.start()
    copies[0].wait()
    copies[1].wait()
    out[0:3, :] = head[0]
    out[3:4, :] = head[1, 0:1]
    out[4:8, :] = jnp.zeros((4, out.shape[1]), jnp.float32)
    for copy in copies[2:]:
        copy.wait()


def lanes(data, start, count):
    return jnp.concatenate(
        [piece[s, start : start + count, :] for piece in data for s in range(piece.shape[0])], axis=1
    )


def distance_operands(scaled):
    ones = jnp.ones((1, scaled.shape[1]), jnp.float32)
    left, right = [], []
    for k in range(3):
        h, m, l = split3(scaled[k : k + 1])
        left += [-2.0 * h, -2.0 * h, -2.0 * m, -2.0 * m, -2.0 * h, -2.0 * l]
        right += [h, m, h, m, l, h]
    norm = scaled[0:1] * scaled[0:1] + scaled[1:2] * scaled[1:2] + scaled[2:3] * scaled[2:3]
    h, m, l = split3(norm)
    left += [h, m, l, ones, ones, ones]
    right += [ones, ones, ones, h, m, l]
    zeros = jnp.zeros((8, scaled.shape[1]), jnp.float32)
    left = jnp.concatenate(left + [zeros], axis=0)
    right = jnp.concatenate(right + [zeros], axis=0).astype(jnp.bfloat16)
    return left.T.astype(jnp.bfloat16), right


def down(w, kernel_block):
    return lax.dot_general(w, kernel_block, (((1,), (0,)), ((), ())), preferred_element_type=jnp.float32)


def across(kernel_block, w):
    return lax.dot_general(kernel_block, w, (((1,), (1,)), ((), ())), preferred_element_type=jnp.float32)


def block_span(index):
    return pl.ds(pl.multiple_of(index * BLOCK, BLOCK), BLOCK)


def strip_size(old, new):
    return sum(j + 1 for j in range(old, old + new))


def build_strips(old, new, lhs, rhs, weighted, table, field, even, odd):
    count = strip_size(old, new)
    starts = [strip_size(old, k) for k in range(new)]

    def place(k):
        j, i = 0, k
        for step in range(1, new):
            past = k >= starts[step]
            j = jnp.where(past, step, j)
            i = jnp.where(past, k - starts[step], i)
        return j, i

    def distances(k):
        j, i = place(k)
        return lax.dot_general(
            lhs[block_span(j), :], rhs[:, block_span(i)], (((1,), (0,)), ((), ())), preferred_element_type=jnp.float32
        )

    def fill(k, source):
        for r in range(0, BLOCK, 64):
            table[k, r : r + 64, :] = green(source[r : r + 64, :])

    def products(k, valid=None):
        j, i = place(k)
        beside = jnp.where(old + j == i, 0.0, 1.0)
        above, below = weighted[:, block_span(i)], weighted[:, block_span(old + j)]
        if valid is not None:
            valid = jnp.where(valid, 1.0, 0.0)
            beside = beside * valid
            above = above * valid.astype(jnp.bfloat16)
        field[:, block_span(old + j)] += lax.dot_general(
            above, table[k], (((1,), (1,)), ((), ())), preferred_element_type=jnp.float32
        )
        field[:, block_span(i)] += down(below * beside.astype(jnp.bfloat16), table[k])

    field[...] = jnp.zeros_like(field)
    table[0] = jnp.zeros((BLOCK, BLOCK), jnp.bfloat16)
    stage = (even, odd)
    even[...] = distances(0)

    def several(t, carry):
        k = UNROLL * t
        for n in range(UNROLL):
            stage[(n + 1) % 2][...] = distances(jnp.minimum(k + n + 1, count - 1))
            if n == 0:
                products(jnp.maximum(k - 1, 0), k > 0)
            else:
                products(k + n - 1)
            fill(k + n, stage[n % 2])
        return carry

    lax.fori_loop(0, count // UNROLL, several, 0)
    for n, k in enumerate(range(count // UNROLL * UNROLL, count)):
        if k + 1 < count:
            stage[(n + 1) % 2][...] = distances(k + 1)
        if k:
            products(k - 1)
        fill(k, stage[n % 2])
    products(count - 1)


def prepare(old, data, columns, total, lhs, rhs, weighted, before):
    scaled = lanes(data, 0, 3) * TURNS
    left, right = distance_operands(scaled)
    lhs[...] = left
    rhs[:, old * BLOCK :] = right
    weighted[:, old * BLOCK :] = (lanes(data, 8, columns) * (FOUR_PI / total)).astype(jnp.bfloat16)
    if old:
        rhs[:, : old * BLOCK] = before[0][...]
        weighted[:, : old * BLOCK] = before[1][...]
    return scaled


def strips_kernel(pieces, old, new, columns, total, *refs):
    data, refs = refs[:pieces], refs[pieces:]
    before = refs[: 2 if old else 0]
    table, field, rhs, weighted, lhs, even, odd = refs[len(before) :]
    prepare(old, data, columns, total, lhs, rhs, weighted, before)
    build_strips(old, new, lhs, rhs, weighted, table, field, even, odd)


def iterate_kernel(pieces, new, blocks, columns, groups, *refs):
    data, refs = refs[:pieces], refs[pieces:]
    rest, refs = refs[:new], refs[new:]
    toward_ref, before, refs = refs[0], refs[1:3], refs[3:]
    tables, refs = refs[: len(groups)], refs[len(groups) :]
    fields, refs = refs[: len(groups)], refs[len(groups) :]
    density_out, far_out = refs[:2]
    lhs, rhs, weighted, table, field, even, odd, coords, plane, dens, inc = refs[2:]
    total = blocks * BLOCK
    width = data[0].shape[2]
    old = blocks - new
    prepare(old, rest, columns, total, lhs, rhs, weighted, before)
    build_strips(old, new, lhs, rhs, weighted, table, field, even, odd)

    everything = list(data) + list(rest)
    coords[0:3, :] = lanes(everything, 0, 3) * TURNS
    inverse = 1.0 / lanes(everything, 3, 1)
    dens[...] = lanes(everything, 8, columns)
    inc[...] = lanes(everything, 8 + columns, columns)
    for part in fields:
        field[:, : part.shape[1]] += part[...]
    dens[...] = dens[...] - (field[...] + inc[...]) * inverse

    entries = {}
    for (first, count), part in zip(list(groups) + [(old, new)], list(tables) + [table]):
        k = 0
        for j in range(first, first + count):
            for i in range(j + 1):
                entries[j, i] = (part, k)
                k += 1

    def entry(j, i):
        part, k = entries[j, i]
        return part[k]

    toward = toward_ref[...].T
    cell_area = FOUR_PI / total

    def rounded():
        return (dens[...] * cell_area).astype(jnp.bfloat16)

    def part_of(w, b):
        return w[:, b * BLOCK : (b + 1) * BLOCK]

    steps = ITERS - 1
    per_step = -(-blocks // steps)

    def iterate(step, carry):
        w = rounded()
        for k in range(per_step):
            span = block_span(jnp.minimum(step * per_step + k, blocks - 1))
            phase = toward[:, 0:1] * coords[0:1, span] + toward[:, 1:2] * coords[1:2, span]
            phase = phase + toward[:, 2:3] * coords[2:3, span]
            plane[:, span] = cos_turns(phase, 1.0).astype(jnp.bfloat16)
        downs, sides = [None] * blocks, [None] * blocks
        for b in range(blocks):
            top = blocks - 1 - b
            for n in range(max(blocks - b, top)):
                if b + n < blocks:
                    term = down(part_of(w, b + n), entry(b + n, b))
                    downs[b] = term if n == 0 else downs[b] + term
                if n < top:
                    term = across(entry(top, n), part_of(w, n))
                    sides[top] = term if n == 0 else sides[top] + term
        for b in range(blocks):
            total_field = downs[b] if sides[b] is None else downs[b] + sides[b].T
            span = slice(b * BLOCK, (b + 1) * BLOCK)
            dens[:, span] = dens[:, span] - (total_field + inc[:, span]) * inverse[:, span]
        return carry

    lax.fori_loop(0, steps, iterate, 0)
    density_out[...] = dens[:, 0:width]
    far_out[...] = across(rounded(), plane[...])


def replicated_shards(points, density, incident, precond, receivers):
    count_tgt = lax.axis_size("tgt")
    count_src = lax.axis_size("src")
    count_sub = lax.axis_size("sub")
    chips = count_tgt * count_src
    columns, width = density.shape
    names = ("tgt", "src", "sub")
    vmem = pl.BlockSpec(memory_space=pltpu.VMEM)
    rows = receivers.shape[0] // (chips * count_sub)
    inputs = (points, precond[None, :], density, incident, receivers.reshape(-1, rows))
    payload, picked = pl.pallas_call(
        pack_kernel,
        out_shape=(
            jax.ShapeDtypeStruct((8 + 2 * columns, width), jnp.float32),
            jax.ShapeDtypeStruct((1, rows), jnp.int32),
        ),
        in_specs=[pl.BlockSpec(memory_space=pltpu.HBM)] * len(inputs),
        out_specs=(vmem, vmem),
        scratch_shapes=[pltpu.VMEM((2, 3, width), jnp.float32), pltpu.SemaphoreType.DMA((len(inputs),))],
        compiler_params=pltpu.CompilerParams(vmem_limit_bytes=4 * 2**20),
        name="pack",
    )(*(pltpu.with_memory_space_constraint(array, pltpu.HBM) for array in inputs))
    swap = [(0, 1), (1, 0)]
    payload = payload[None]

    def fetch(array, offsets):
        pairs = [(q * 2 + c, (q ^ offsets[c]) * 2 + c) for q in range(chips) for c in range(2)]
        return lax.ppermute(array, names, pairs)

    far = fetch(payload, (chips - 1, chips - 1))
    own = jnp.concatenate([payload, lax.ppermute(payload, "sub", swap)], axis=0)
    near = [fetch(own, (k, k + 1)) for k in range(1, chips - 1, 2)]

    toward = receiver_directions(picked[0])
    toward = jnp.concatenate([toward, jnp.zeros((5, rows), jnp.float32)], axis=0)

    blocks = chips
    total = blocks * BLOCK
    f32, bf16 = jnp.float32, jnp.bfloat16

    def strip_shapes(old, new):
        return [
            ((strip_size(old, new), BLOCK, BLOCK), bf16),
            ((columns, (old + new) * BLOCK), f32),
            ((32, (old + new) * BLOCK), bf16),
            ((columns, (old + new) * BLOCK), bf16),
            ((new * BLOCK, 32), bf16),
            ((BLOCK, BLOCK), f32),
            ((BLOCK, BLOCK), f32),
        ]

    groups, tables, fields, held, before = [], [], [], [], []

    def strips(data):
        old, new = (sum(array.shape[0] for array in arrays) // 2 for arrays in (held, data))
        shapes = strip_shapes(old, new)
        work = strip_size(old, new) * BLOCK * BLOCK
        table, field, *state = pl.pallas_call(
            functools.partial(strips_kernel, len(data), old, new, columns, total),
            out_shape=[jax.ShapeDtypeStruct(*shape) for shape in shapes[:4]],
            in_specs=[vmem] * (len(data) + len(before)),
            out_specs=[vmem] * 4,
            scratch_shapes=[pltpu.VMEM(*shape) for shape in shapes[4:]],
            compiler_params=pltpu.CompilerParams(vmem_limit_bytes=VMEM_LIMIT),
            cost_estimate=pl.CostEstimate(flops=30 * work, bytes_accessed=2 * work, transcendentals=2 * work),
            name=f"strips{old}",
        )(*data, *before)
        groups.append((old, new))
        tables.append(table)
        fields.append(field)
        held.extend(data)
        before[:] = state

    def both(array):
        return [array, lax.ppermute(array, "sub", swap)]

    def swapped(array):
        return lax.ppermute(array, "sub", swap)

    first, late = [own, far, swapped(far)], near
    if len(near) > 1:
        first[1:1] = [near[0], swapped(near[0])]
        late = near[1:]
    strips(first)
    *late, fields[0] = lax.optimization_barrier((*late, fields[0]))
    rest = [swapped(array) for array in late]
    strips(late)
    pieces, new = len(held), len(rest)
    shapes = strip_shapes(blocks - new, new)
    return pl.pallas_call(
        functools.partial(iterate_kernel, pieces, new, blocks, columns, tuple(groups)),
        out_shape=(
            jax.ShapeDtypeStruct((columns, width), f32),
            jax.ShapeDtypeStruct((columns, rows), f32),
        ),
        in_specs=[vmem] * (pieces + new + 3 + 2 * len(groups)),
        out_specs=(vmem, vmem),
        scratch_shapes=[pltpu.VMEM(*shapes[k]) for k in (4, 2, 3, 0, 1, 5, 6)]
        + [
            pltpu.VMEM((8, total), f32),
            pltpu.VMEM((rows, total), bf16),
            pltpu.VMEM((columns, total), f32),
            pltpu.VMEM((columns, total), f32),
        ],
        compiler_params=pltpu.CompilerParams(vmem_limit_bytes=VMEM_LIMIT),
        name="iterate",
    )(*held, *rest, toward, *before, *tables, *fields)


def single_layer(targets, sources):
    delta_x = targets[0][:, None] - sources[0][None, :]
    delta_y = targets[1][:, None] - sources[1][None, :]
    delta_z = targets[2][:, None] - sources[2][None, :]
    squared = delta_x * delta_x + delta_y * delta_y + delta_z * delta_z
    values = jnp.cos(WAVENUMBER * jnp.sqrt(squared)) / (
        FOUR_PI * jnp.sqrt(squared + SMOOTHING * SMOOTHING)
    )
    return values.astype(jnp.bfloat16)


def far_kernel(toward, sources):
    projection = toward[0][:, None] * sources[0][None, :] + toward[1][:, None] * sources[1][None, :]
    projection = projection + toward[2][:, None] * sources[2][None, :]
    return jnp.cos(WAVENUMBER * projection).astype(jnp.bfloat16)


def receiver_directions(direction_index):
    upper_part = direction_index // 256
    lower_part = direction_index % 256
    rotation = (upper_part * 14080 + lower_part * 40503) % 65536
    azimuth = rotation.astype(jnp.float32) * (2.0 * math.pi / 65536.0)
    height = 1.0 - (2 * direction_index + 1).astype(jnp.float32) / NDIR
    radial = jnp.sqrt(jnp.maximum(1.0 - height * height, 0.0))
    return jnp.stack([radial * jnp.cos(azimuth), radial * jnp.sin(azimuth), height])


def fold_blocks(running, incoming, coordinates, targets, maker):
    length = incoming.shape[1]
    block_width = math.gcd(length, 1024)

    def fold_one_block(number, accumulated):
        inside = number * block_width
        part_density = lax.dynamic_slice_in_dim(incoming, inside, block_width, 1)
        part_points = lax.dynamic_slice_in_dim(coordinates, inside, block_width, 1)
        kernel_table = maker(targets, part_points)
        return accumulated + lax.dot_general(
            part_density, kernel_table, (((1,), (1,)), ((), ())), preferred_element_type=jnp.float32
        )

    return lax.fori_loop(0, length // block_width, fold_one_block, running)


def build_table(targets, sources):
    source_count = sources.shape[1]
    block_width = math.gcd(source_count, 1024)
    table = jnp.zeros((targets.shape[1], source_count), jnp.bfloat16)

    def build_one_block(number, filled):
        inside = number * block_width
        part_points = lax.dynamic_slice_in_dim(sources, inside, block_width, 1)
        return lax.dynamic_update_slice_in_dim(
            filled, single_layer(targets, part_points), inside, 1
        )

    return lax.fori_loop(0, source_count // block_width, build_one_block, table)


def shared_shards(points, density, incident, precond, receivers):
    count_tgt = lax.axis_size("tgt")
    count_src = lax.axis_size("src")
    count_sub = lax.axis_size("sub")
    point_count = points.shape[1] * count_tgt * count_src * count_sub
    cell_area = FOUR_PI / point_count
    row_points = lax.all_gather(points, "src", axis=1, tiled=True)
    column_points = lax.all_gather(points, ("tgt", "sub"), axis=1, tiled=True)
    columns_count = density.shape[0]
    stored_table = build_table(row_points, column_points)
    for iteration in range(ITERS):
        weighted = (density * cell_area).astype(jnp.bfloat16)
        partial_sum = lax.dot_general(
            lax.all_gather(weighted, ("tgt", "sub"), axis=1, tiled=True),
            stored_table,
            (((1,), (1,)), ((), ())),
            preferred_element_type=jnp.float32,
        )
        field = lax.psum_scatter(partial_sum, "src", scatter_dimension=1, tiled=True)
        density = density - (field + incident) / precond[None, :]
    weighted = (density * cell_area).astype(jnp.bfloat16)
    receiver_blocks = receivers.reshape(count_tgt, count_src, count_sub, -1)
    picked = lax.dynamic_index_in_dim(receiver_blocks, lax.axis_index("tgt"), 0, keepdims=False)
    picked = lax.dynamic_index_in_dim(picked, lax.axis_index("sub"), 1, keepdims=False)
    toward = receiver_directions(picked.reshape(-1))
    empty_far = jnp.zeros((columns_count, toward.shape[1]), jnp.float32)
    far_partial = fold_blocks(
        empty_far,
        lax.all_gather(weighted, ("tgt", "sub"), axis=1, tiled=True),
        column_points,
        toward,
        far_kernel,
    )
    far_field = lax.psum_scatter(far_partial, "src", scatter_dimension=1, tiled=True)
    return (density, far_field)


def can_replicate(mesh, points):
    sizes = mesh.shape
    chips = sizes["tgt"] * sizes["src"]
    per_group = chips * sizes["sub"]
    total = points.shape[1] // sizes["groups"]
    return (
        sizes["sub"] == 2
        and chips >= 4
        and chips & (chips - 1) == 0
        and total == per_group * (BLOCK // 2)
        and total * total <= TABLE_LIMIT
    )


def solution(mesh):
    placed = (
        P(None, ("groups", "tgt", "src", "sub")),
        P(None, ("groups", "tgt", "src", "sub")),
        P(None, ("groups", "tgt", "src", "sub")),
        P(("groups", "tgt", "src", "sub")),
        P("groups"),
    )

    def whole(points, density, incident, precond, receivers):
        body = replicated_shards if can_replicate(mesh, points) else shared_shards
        return jax.shard_map(
            body,
            mesh=mesh,
            in_specs=placed,
            out_specs=(
                P(None, ("groups", "tgt", "src", "sub")),
                P(None, ("groups", "tgt", "src", "sub")),
            ),
            check_vma=False,
        )(points, density, incident, precond, receivers)

    return whole
```
